32 devices in a mesh: grp: 2 (over x), cell: 16 (over z, y, core).
Axes of the slice: x: 2, y: 2, z: 4, core: 2. Of those that a mesh axis runs over, the one named last changes fastest.
Arguments:
- features: float32 [8192, 256], P(('grp', 'cell')), parts along dimension 0, may hold values from -6 to 6
- counts: int32 [32], P(('grp', 'cell')), parts along dimension 0, may hold values from 1 to 256, 3072 in all
- cotangent: float32 [2, 8192], P(None, ('grp', 'cell')), parts along dimension 1, may hold values from -6 to 6
- weight_in: float32 [2, 256, 512], replicated, may hold values from -0.375 to 0.375
- weight_temp: float32 [2, 32], replicated, may hold values from -1 to 1
- weight_slice: float32 [2, 32, 64], replicated, may hold values from -1 to 1
- weight_qkv: float32 [2, 32, 96], replicated, may hold values from -1 to 1
- weight_out: float32 [2, 256, 256], replicated, may hold values from -0.375 to 0.375
- expansion_matrix: float32 [2, 256, 1024], replicated, may hold values from -0.375 to 0.375
- weight_down: float32 [2, 1024, 256], replicated, may hold values from -0.1875 to 0.1875
- weight_head: float32 [256, 2], replicated, may hold values from -0.375 to 0.375
Outputs:
- prediction: float32 [2, 8192], P(None, ('grp', 'cell')), parts along dimension 1
- grad_in: float32 [4, 256, 512], P('grp'), parts along dimension 0
- grad_temp: float32 [4, 32], P('grp'), parts along dimension 0
- grad_slice: float32 [4, 32, 64], P('grp'), parts along dimension 0
- grad_qkv: float32 [4, 32, 96], P('grp'), parts along dimension 0
- grad_out: float32 [4, 256, 256], P('grp'), parts along dimension 0
- grad_up: float32 [4, 256, 1024], P('grp'), parts along dimension 0
- grad_down: float32 [4, 1024, 256], P('grp'), parts along dimension 0
- grad_head: float32 [512, 2], P('grp'), parts along dimension 0
The draws below stay inside these ranges and needn't reach their ends.
There are 2 independent parts, one for each index of `grp`. The reference program is written for one: setup_inputs(seed, part) draws one part's arguments, and reference() takes and returns one part's arrays. A program takes and returns all parts, laid end to end along the dimension named above; an argument that names none is the same for every part. Nothing has to cross between parts.
Inputs may be any that keep to these rules, and one draw needn't show every extreme that they name: counts[b] is the number of live cell slots of device block b; they sum to 3072, and the largest is 256.
All inputs are finite; a program needn't handle non-finite values.
Results may differ from the reference program's by a relative error of at most 0.0003.
Values sent between devices are 32-bit elements; how exact they have to be, the bound alone decides.
No kernel may reach another device: no remote copies, remote signals or barrier semaphores. Data moves between devices by JAX's collectives and lax.ppermute only.
A program may use at most 128 MiB of HBM per device.

```python
import math
import jax
import jax.numpy as jnp
import numpy as np
from jax import lax

D = 256
H = 8
M = 64
FF = 1024
L = 2
ELEMENTS_PER_GPU = 256
DH = 32
CELLS = 4096
LIVE = 3072
N_CELL = 16


def levels(rng, dims, shards, least, top_value):
    factor_of = 1.0
    for position, blocks in shards:
        heights = jax.random.uniform(jax.random.fold_in(jax.random.fold_in(rng, 6), position), (blocks,), jnp.float32, least / len(shards), top_value / len(shards))
        factor_of = factor_of * jnp.repeat(jnp.exp(heights), dims[position] // blocks).reshape((-1,) + (1,) * (len(dims) - 1 - position))
    return factor_of


def length_profile(count, total, limit, skew):
    loads = [(1 << 20) // math.isqrt(standing ** skew) + 1 for standing in range(2, count + 1)]
    spare, given = total - limit - (count - 1), [1] * (count - 1)
    while spare > 0:
        movable = [i for i in range(count - 1) if given[i] < limit]
        whole, remaining = sum([loads[i] for i in movable]), spare
        for i in movable:
            extra = min(limit - given[i], max(1, remaining * loads[i] // whole), spare)
            given[i] = given[i] + extra
            spare = spare - extra
    return np.array([limit] + given)


def ragged(key, amount, total, reach, slope):
    if amount == 2:
        one = jax.random.randint(key, (), max(1, total - reach), min(reach, total - 1) + 1)
        return jnp.stack([one, total - one])
    sizes = jnp.asarray(length_profile(amount, total, reach, slope), jnp.int32)
    twos = (amount - 1) // 2
    source_of, taker = sizes[1:1 + 2 * twos:2], sizes[2:2 + 2 * twos:2]
    margin = jnp.minimum(source_of - 1, reach - taker)
    shifted = jax.random.randint(jax.random.fold_in(key, 1), (twos,), 0, 1 << 20) % (margin + 1)
    sizes = sizes.at[1:1 + 2 * twos:2].set(source_of - shifted).at[2:2 + 2 * twos:2].set(taker + shifted)
    return sizes[jax.random.permutation(jax.random.fold_in(key, 2), amount)]


def gaussian(rng, extent, scale, limit, split=(), kind=jnp.bfloat16):
    array = jax.random.normal(rng, extent, jnp.float32) * scale
    if len(split) > 0:
        array = levels(rng, extent, split, -0.22, 0.18) * array
    return jnp.clip(array, min=-limit, max=limit).astype(kind)


def setup_inputs(seed: int = 0, part: int = 0) -> dict:
    arg_keys = jax.random.split(jax.random.key(seed), 12)
    part_keys = jax.random.split(jax.random.fold_in(arg_keys[11], part), 12)
    features = gaussian(part_keys[0], (CELLS, D), 1.0, 6.0, ((0, 16),), jnp.float32)
    counts = ragged(part_keys[1], N_CELL, LIVE, ELEMENTS_PER_GPU, 2).astype(jnp.int32)
    cotangent = gaussian(part_keys[2], (2, CELLS), 1.0, 6.0, ((1, 16),), jnp.float32)
    weight_in = gaussian(arg_keys[3], (L, D, 2 * D), D ** -0.5, 0.375, (), jnp.float32)
    weight_temp = gaussian(arg_keys[4], (L, DH), DH ** -0.5, 1.0, (), jnp.float32)
    weight_slice = gaussian(arg_keys[5], (L, DH, M), DH ** -0.5, 1.0, (), jnp.float32)
    weight_qkv = gaussian(arg_keys[6], (L, DH, 3 * DH), DH ** -0.5, 1.0, (), jnp.float32)
    weight_out = gaussian(arg_keys[7], (L, D, D), D ** -0.5, 0.375, (), jnp.float32)
    expansion_matrix = gaussian(arg_keys[8], (L, D, FF), D ** -0.5, 0.375, (), jnp.float32)
    weight_down = gaussian(arg_keys[9], (L, FF, D), FF ** -0.5, 0.1875, (), jnp.float32)
    weight_head = gaussian(arg_keys[10], (D, 2), D ** -0.5, 0.375, (), jnp.float32)
    return dict(features=features, counts=counts, cotangent=cotangent, weight_in=weight_in, weight_temp=weight_temp, weight_slice=weight_slice, weight_qkv=weight_qkv, weight_out=weight_out, expansion_matrix=expansion_matrix, weight_down=weight_down, weight_head=weight_head)


strict_reference_switch = lax.Precision.HIGHEST
epsilon = 1e-05

def matmul(left, right):
    return jnp.dot(left, right, precision=strict_reference_switch, preferred_element_type=jnp.float32)

def normalize(field):
    average = lax.optimization_barrier(jnp.mean(field, axis=-1, keepdims=True))
    centered = field - average
    variance = lax.optimization_barrier(jnp.mean(centered * centered, axis=-1, keepdims=True))
    return centered * lax.rsqrt(variance + 1e-05)

def front(field, w_in, w_temp, w_slice, mask):
    element_total_number, model_width = field.shape
    projected = matmul(normalize(field), w_in)
    x_mid = projected[:, :model_width].reshape(element_total_number, H, -1)
    features = projected[:, model_width:].reshape(element_total_number, H, -1)
    temper = 0.5 + jax.nn.softplus(jnp.einsum('nhd,d->nh', x_mid, w_temp, precision=strict_reference_switch))
    logits = jnp.einsum('nhd,dm->nhm', x_mid, w_slice, precision=strict_reference_switch) / temper[:, :, None]
    exponent = jnp.exp(logits)
    normalized_assignment_probabilities = exponent / lax.optimization_barrier(jnp.sum(exponent, axis=-1, keepdims=True)) * mask[:, None, None]
    numerator = jnp.einsum('wes,wek->esk', normalized_assignment_probabilities, features, precision=strict_reference_switch)
    denom = lax.optimization_barrier(jnp.sum(normalized_assignment_probabilities, axis=0))
    return (normalized_assignment_probabilities, numerator, denom)

def middle(token_states, query_key_value_weight):
    head_width = token_states.shape[-1]
    query_key_value = jnp.einsum('kwz,za->kwa', token_states, query_key_value_weight, precision=strict_reference_switch)
    query_rows = query_key_value[:, :, :head_width]
    key_portion = query_key_value[:, :, head_width:2 * head_width]
    value_portion = query_key_value[:, :, 2 * head_width:]
    attention_scores = jnp.einsum('gus,gvs->guv', query_rows, key_portion, precision=strict_reference_switch) / jnp.sqrt(jnp.float32(head_width))
    exponent = jnp.exp(attention_scores)
    attention_map = exponent / lax.optimization_barrier(jnp.sum(exponent, axis=-1, keepdims=True))
    return jnp.einsum('juz,jzq->juq', attention_map, value_portion, precision=strict_reference_switch)

def rear(field, normalized_assignment_probabilities, blended_points, w_out, w_up, w_down):
    element_total_number = field.shape[0]
    restored_point_features = jnp.einsum('wel,elu->weu', normalized_assignment_probabilities, blended_points, precision=strict_reference_switch).reshape(element_total_number, -1)
    first = field + matmul(restored_point_features, w_out)
    hidden = jax.nn.gelu(matmul(normalize(first), w_up), approximate=True)
    return first + matmul(hidden, w_down)

def readout(field, w_head):
    return matmul(normalize(field), w_head).T

def reference(features, counts, cotangent, weight_in, weight_temp, weight_slice, weight_qkv, weight_out, expansion_matrix, weight_down, weight_head):
    element_total_number = features.shape[0]
    index = jnp.arange(element_total_number, dtype=jnp.int32)
    block = index // ELEMENTS_PER_GPU
    mask = (index % ELEMENTS_PER_GPU < counts[block]).astype(jnp.float32)

    def forward(w_in, w_temp, w_slice, query_key_value_weight, w_out, w_up, w_down, w_head):
        field = features
        for layer in range(L):
            normalized_assignment_probabilities, numerator, denom = front(field, w_in[layer], w_temp[layer], w_slice[layer], mask)
            token_states = numerator / (denom[:, :, None] + epsilon)
            blended_points = middle(token_states, query_key_value_weight[layer])
            field = rear(field, normalized_assignment_probabilities, blended_points, w_out[layer], w_up[layer], w_down[layer])
        return readout(field, w_head)
    prediction, pullback = jax.vjp(forward, weight_in, weight_temp, weight_slice, weight_qkv, weight_out, expansion_matrix, weight_down, weight_head)
    grads = pullback(cotangent * mask[None, :])
    return (prediction, grads[0], grads[1], grads[2], grads[3], grads[4], grads[5], grads[6], grads[7])
```

```python
from functools import partial

import jax
import jax.numpy as jnp
from jax import lax
from jax.experimental import pallas as pl
from jax.experimental.pallas import tpu as pltpu
from jax.sharding import PartitionSpec as P

H = 8
L = 2
F32 = jnp.float32
BF16 = jnp.bfloat16
EPS = 1e-05


def split(a):
    if isinstance(a, tuple):
        return a
    hi = a.astype(BF16)
    return hi, (a - hi.astype(F32)).astype(BF16)


def exact(a):
    return (a.astype(BF16),)


def raw(a, b, ca, cb):
    return lax.dot_general(a, b, (((ca,), (cb,)), ((), ())), preferred_element_type=F32)


def product(a, b, ca, cb):
    a, b = split(a), split(b)
    out = raw(a[0], b[0], ca, cb)
    if len(b) > 1:
        out = out + raw(a[0], b[1], ca, cb)
    if len(a) > 1:
        out = out + raw(a[1], b[0], ca, cb)
    return out


def nn(a, b):
    return product(a, b, 1, 0)


def nt(a, b):
    return product(a, b, 1, 1)


def tn(a, b):
    return product(a, b, 0, 0)


def same_head(rows, row_head, cols, col_head):
    r = lax.broadcasted_iota(jnp.int32, (rows, cols), 0) // row_head
    c = lax.broadcasted_iota(jnp.int32, (rows, cols), 1) // col_head
    return r == c


def ones_block(rows, row_head, cols, col_head):
    return exact(same_head(rows, row_head, cols, col_head).astype(F32))


def expand(small, col_head):
    r, cols = small.shape
    tiled = jnp.concatenate([small] * H, axis=0)
    return jnp.where(same_head(H * r, r, cols, col_head), tiled, 0.0)


def fold(dense, col_head):
    rows, cols = dense.shape
    r = rows // H
    head = lax.broadcasted_iota(jnp.int32, (r, cols), 1) // col_head
    out = jnp.where(head == 0, dense[:r], 0.0)
    for h in range(1, H):
        out = jnp.where(head == h, dense[h * r : (h + 1) * r], out)
    return out


def tile_lanes(a, times):
    return jnp.concatenate([a] * times, axis=1)


def norm(field):
    centered = field - jnp.mean(field, axis=-1, keepdims=True)
    rstd = lax.rsqrt(jnp.mean(centered * centered, axis=-1, keepdims=True) + EPS)
    return centered * rstd, rstd


def norm_back(dy, y, rstd):
    return rstd * (
        dy - jnp.mean(dy, axis=-1, keepdims=True) - y * jnp.mean(dy * y, axis=-1, keepdims=True)
    )


def softplus(t):
    return jnp.maximum(t, 0.0) + jnp.log(1.0 + jnp.exp(-jnp.abs(t)))


def front(field, w_in, w_temp, w_slice, live):
    n, width = field.shape
    dh, m = w_slice.shape
    hm = H * m
    nf, rstd = norm(field)
    proj = nn(nf, w_in)
    x, v = proj[:, :width], proj[:, width:]
    wt = tile_lanes(w_temp, H)
    xt = split(x * wt)
    t_wide = nn(xt, ones_block(width, dh, hm, m))
    t_slim = nn(xt, ones_block(width, dh, width, dh))
    r = 1.0 / (0.5 + softplus(t_wide))
    rs = jax.nn.sigmoid(t_slim) / (0.5 + softplus(t_slim))
    logits = nn(x, expand(tile_lanes(w_slice, H), m)) * r
    e = jnp.exp(logits)
    z = nn(e, ones_block(hm, m, hm, m))
    rows = lax.broadcasted_iota(jnp.int32, (n, hm), 0)
    s = jnp.where(rows < live, e / z, 0.0)
    numer = fold(tn(v, s), m)
    denom = jnp.sum(s, axis=0, keepdims=True)
    packed = jnp.concatenate([numer, jnp.broadcast_to(denom, (8, hm))], axis=0)
    return packed, s, proj, nf, rstd, logits, r, rs


def tokens_of(packed, dh):
    inv = 1.0 / (packed[dh : dh + 1] + EPS)
    return packed[:dh] * inv, inv


def middle(packed, w_qkv):
    dh = w_qkv.shape[0]
    tok, inv = tokens_of(packed, dh)
    qkv = tn(w_qkv, tok)
    q, k, v = qkv[:dh], qkv[dh : 2 * dh], qkv[2 * dh :]
    hm = tok.shape[1]
    m = hm // H
    pair = 2 * m
    own = same_head(pair, m, pair, m)
    scale = 1.0 / float(dh) ** 0.5
    maps, mixed = [], []
    for g in range(H // 2):
        lanes = slice(g * pair, (g + 1) * pair)
        e = jnp.where(own, jnp.exp(tn(k[:, lanes], q[:, lanes]) * scale), 0.0)
        a = e / jnp.sum(e, axis=0, keepdims=True)
        maps.append(a)
        mixed.append(nn(v[:, lanes], a))
    return tok, inv, q, k, v, maps, jnp.concatenate(mixed, axis=1)


def middle_back(packed, w_qkv, d_mixed):
    dh = w_qkv.shape[0]
    tok, inv, q, k, v, maps, _ = middle(packed, w_qkv)
    hm = tok.shape[1]
    pair = 2 * (hm // H)
    scale = 1.0 / float(dh) ** 0.5
    dq, dk, dv = [], [], []
    for g in range(H // 2):
        lanes = slice(g * pair, (g + 1) * pair)
        a, dm = maps[g], d_mixed[:, lanes]
        dv.append(nt(dm, a))
        da = tn(v[:, lanes], dm)
        ds = a * (da - jnp.sum(a * da, axis=0, keepdims=True)) * scale
        dk.append(nt(q[:, lanes], ds))
        dq.append(nn(k[:, lanes], ds))
    d_qkv = jnp.concatenate([jnp.concatenate(p, axis=1) for p in (dq, dk, dv)], axis=0)
    g_qkv = nt(tok, d_qkv)
    d_tok = nn(w_qkv, d_qkv)
    d_numer = d_tok * inv
    d_denom = -jnp.sum(d_tok * tok, axis=0, keepdims=True) * inv
    return g_qkv, d_numer, d_denom


def front_back(ds, d_numer, d_denom, s, proj, nf, logits, r, rs, w_in, w_temp, w_slice):
    width = proj.shape[1] // 2
    dh, m = w_slice.shape
    hm = H * m
    x, v = proj[:, :width], proj[:, width:]
    d_blk = split(expand(d_numer, m))
    ds = ds + nn(v, d_blk) + d_denom
    dv = nt(s, d_blk)
    sds = s * ds
    d_logits = sds - s * nn(sds, ones_block(hm, m, hm, m))
    d_t = -rs * nn(d_logits * logits, ones_block(hm, m, width, dh))
    du = split(d_logits * r)
    wt = tile_lanes(w_temp, H)
    dx = nt(du, expand(tile_lanes(w_slice, H), m)) + d_t * wt
    g_temp = jnp.sum(x * d_t, axis=0, keepdims=True)
    g_slice = fold(tn(x, du), m)
    g_slice = sum(g_slice[:, g * 2 * m : (g + 1) * 2 * m] for g in range(H // 2))
    g_slice = g_slice[:, :m] + g_slice[:, m:]
    d_proj = split(jnp.concatenate([dx, dv], axis=1))
    g_in = tn(nf, d_proj)
    return d_proj, g_in, g_temp, g_slice


def gelu_parts(pre):
    c = 0.7978845608028654
    sq = pre * pre
    t = jnp.tanh(c * pre * (1.0 + 0.044715 * sq))
    hid = 0.5 * pre * (1.0 + t)
    slope = 0.5 * (1.0 + t) + 0.5 * pre * (1.0 - t * t) * c * (1.0 + 3 * 0.044715 * sq)
    return hid, slope


def rear(field, s, mixed, w_out, w_up, w_down):
    m = mixed.shape[1] // H
    des = nt(s, expand(mixed, m))
    first = field + nn(des, w_out)
    n1, rstd1 = norm(first)
    pre = nn(n1, w_up)
    hid, _ = gelu_parts(pre)
    return first + nn(hid, w_down), des, n1, rstd1, pre


def rear_back(g, s, mixed, des, n1, rstd1, pre, w_out, w_up, w_down):
    m = mixed.shape[1] // H
    hid, slope = gelu_parts(pre)
    gs = split(g)
    g_down = tn(hid, gs)
    d_pre = split(nt(gs, w_down) * slope)
    g_up = tn(n1, d_pre)
    d_first = g + norm_back(nt(d_pre, w_up), n1, rstd1)
    dfs = split(d_first)
    g_out = tn(des, dfs)
    d_des = split(nt(dfs, w_out))
    ds = nn(d_des, expand(mixed, m))
    d_mixed = fold(tn(d_des, s), m)
    return d_first, ds, d_mixed, g_out, g_up, g_down


def store(refs, values):
    for ref, value in zip(refs, values, strict=True):
        ref[...] = value


def kernel_a(live, field, w_in, w_temp, w_slice, *out):
    store(out, front(field[...], w_in[...], w_temp[...], w_slice[...], live[0]))


def kernel_b(live, packed, field, s, w_qkv, w_out, w_up, w_down, w_in, w_temp, w_slice, *out):
    mixed = middle(packed[...], w_qkv[...])[-1]
    f1, des, n1, rstd1, pre = rear(field[...], s[...], mixed, w_out[...], w_up[...], w_down[...])
    store(out[:5], (mixed, des, n1, rstd1, pre))
    out[5][...] = f1
    store(out[6:], front(f1, w_in[...], w_temp[...], w_slice[...], live[0]))


def kernel_c(live, packed, field, s, w_qkv, w_out, w_up, w_down, w_head, cot, *out):
    pred, g_head, d_first, ds, d_mixed, g_out, g_up, g_down = out
    n = field.shape[0]
    mixed = middle(packed[...], w_qkv[...])[-1]
    s = s[...]
    f2, des, n1, rstd1, pre = rear(field[...], s, mixed, w_out[...], w_up[...], w_down[...])
    n2, rstd2 = norm(f2)
    wh = w_head[...]
    n2s = split(n2)
    pred[...] = nt(wh, n2s)[:2]
    lanes = lax.broadcasted_iota(jnp.int32, cot.shape, 1)
    dp = jnp.where(lanes < live[0], cot[...], 0.0)
    dp = jnp.concatenate([dp, jnp.zeros((6, n), F32)], axis=0)
    g_head[...] = nn(dp, n2s)
    g = norm_back(tn(dp, wh), n2, rstd2)
    store(
        (d_first, ds, d_mixed, g_out, g_up, g_down),
        rear_back(g, s, mixed, des, n1, rstd1, pre, w_out[...], w_up[...], w_down[...]),
    )


def kernel_d(
    packed, d_mixed, w_qkv, d_first, ds, s, proj, nf, rstd, logits, r, rs, w_in, w_temp, w_slice,
    s0, mixed0, des0, n10, rstd10, pre0, w_out0, w_up0, w_down0, *out,
):
    g_qkv, d_numer, d_denom = middle_back(packed[...], w_qkv[...], d_mixed[...])
    d_proj, g_in, g_temp, g_slice = front_back(
        ds[...], d_numer, d_denom, s[...], proj[...], nf[...], logits[...], r[...], rs[...],
        w_in[...], w_temp[...], w_slice[...],
    )
    store(out[:4], (g_qkv, g_in, g_temp, g_slice))
    g = d_first[...] + norm_back(nt(d_proj, w_in[...]), nf[...], rstd[...])
    _, ds0, d_mixed0, g_out, g_up, g_down = rear_back(
        g, s0[...], mixed0[...], des0[...], n10[...], rstd10[...], pre0[...],
        w_out0[...], w_up0[...], w_down0[...],
    )
    store(out[4:], (ds0, d_mixed0, g_out, g_up, g_down))


def kernel_e(packed, d_mixed, w_qkv, ds, s, proj, nf, logits, r, rs, w_in, w_temp, w_slice, *out):
    g_qkv, d_numer, d_denom = middle_back(packed[...], w_qkv[...], d_mixed[...])
    _, g_in, g_temp, g_slice = front_back(
        ds[...], d_numer, d_denom, s[...], proj[...], nf[...], logits[...], r[...], rs[...],
        w_in[...], w_temp[...], w_slice[...],
    )
    store(out, (g_qkv, g_in, g_temp, g_slice))


VM = pl.BlockSpec(memory_space=pltpu.VMEM)
SM = pl.BlockSpec(memory_space=pltpu.SMEM)


def call(body, shapes, *args, name):
    specs = [SM if a.dtype == jnp.int32 else VM for a in args]
    return pl.pallas_call(
        body,
        out_shape=[jax.ShapeDtypeStruct(s, F32) for s in shapes],
        in_specs=specs,
        out_specs=[VM] * len(shapes),
        compiler_params=pltpu.CompilerParams(vmem_limit_bytes=56 * 1024 * 1024),
        name=name,
    )(*args)


def swap(a, bit, count):
    return lax.ppermute(a, "cell", [(i, i ^ bit) for i in range(count)])


def sum_small(a, count):
    a = a + swap(a, 1, count)
    bit = 2
    while bit < count:
        if 2 * bit < count:
            one, two, both = (swap(a, b, count) for b in (bit, 2 * bit, 3 * bit))
            a = (a + one) + (two + both)
            bit *= 4
        else:
            a = a + swap(a, bit, count)
            bit *= 2
    return a


def shards(
    count,
    features,
    counts,
    cotangent,
    weight_in,
    weight_temp,
    weight_slice,
    weight_qkv,
    weight_out,
    expansion_matrix,
    weight_down,
    weight_head,
):
    n, width = features.shape
    dh, m = weight_slice.shape[1:]
    ff = expansion_matrix.shape[2]
    hm = H * m
    wi = [weight_in[l] for l in range(L)]
    wt = [weight_temp[l : l + 1] for l in range(L)]
    ws = [weight_slice[l] for l in range(L)]
    wq = [weight_qkv[l] for l in range(L)]
    wo = [weight_out[l] for l in range(L)]
    wu = [expansion_matrix[l] for l in range(L)]
    wd = [weight_down[l] for l in range(L)]
    wh = jnp.pad(weight_head.T, ((0, 6), (0, 0)))

    front_shapes = [
        (dh + 8, hm), (n, hm), (n, 2 * width), (n, width), (n, 1), (n, hm), (n, hm), (n, width),
    ]
    rear_shapes = [(dh, hm), (n, width), (n, width), (n, 1), (n, ff)]
    grad_rear = [(width, width), (width, ff), (ff, width)]
    grad_front = [(dh, 3 * dh), (width, 2 * width), (1, width), (dh, m)]

    p0, s0, proj0, nf0, _, lg0, r0, rs0 = call(
        kernel_a, front_shapes, counts, features, wi[0], wt[0], ws[0], name="front0"
    )
    p0 = sum_small(p0, count)
    mix0, des0, n10, rd10, pre0, f1, p1, s1, proj1, nf1, rstd1, lg1, r1, rs1 = call(
        kernel_b, rear_shapes + [(n, width)] + front_shapes,
        counts, p0, features, s0, wq[0], wo[0], wu[0], wd[0], wi[1], wt[1], ws[1], name="rear0_front1",
    )
    p1 = sum_small(p1, count)
    pred, g_head, d_first, ds1, dm1, go1, gu1, gd1 = call(
        kernel_c, [(2, n), (8, width), (n, width), (n, hm), (dh, hm)] + grad_rear,
        counts, p1, f1, s1, wq[1], wo[1], wu[1], wd[1], wh, cotangent, name="rear1_head_back1",
    )
    dm1 = sum_small(dm1, count)
    gq1, gi1, gt1, gs1, ds0, dm0, go0, gu0, gd0 = call(
        kernel_d, grad_front + [(n, hm), (dh, hm)] + grad_rear,
        p1, dm1, wq[1], d_first, ds1, s1, proj1, nf1, rstd1, lg1, r1, rs1, wi[1], wt[1], ws[1],
        s0, mix0, des0, n10, rd10, pre0, wo[0], wu[0], wd[0], name="back_front1_rear0",
    )
    dm0 = sum_small(dm0, count)
    gq0, gi0, gt0, gs0 = call(
        kernel_e, grad_front,
        p0, dm0, wq[0], ds0, s0, proj0, nf0, lg0, r0, rs0, wi[0], wt[0], ws[0], name="back_front0",
    )
    pair = lambda a, b: jnp.stack([a, b])
    big = lax.psum(
        (pair(gi0, gi1), pair(go0, go1), pair(gu0, gu1), pair(gd0, gd1)), "cell"
    )
    gt, gs, gh = (
        sum_small(a, count)
        for a in (jnp.concatenate([gt0, gt1], axis=0), pair(gs0, gs1), g_head)
    )
    gt = gt.reshape(L, H, dh).sum(1)
    return (
        pred, big[0], gt, gs, pair(gq0, gq1), big[1], big[2], big[3], gh[:2].T,
    )


def solution(mesh):
    cells = P(("grp", "cell"))
    return jax.shard_map(
        partial(shards, mesh.shape["cell"]),
        mesh=mesh,
        in_specs=(P(("grp", "cell"), None), cells, P(None, ("grp", "cell"))) + (P(),) * 8,
        out_specs=(
            P(None, ("grp", "cell")),
            P("grp", None, None),
            P("grp", None),
            P("grp", None, None),
            P("grp", None, None),
            P("grp", None, None),
            P("grp", None, None),
            P("grp", None, None),
            P("grp", None),
        ),
        check_vma=False,
    )
```

```python
from functools import partial

import jax
import jax.numpy as jnp
from jax import lax
from jax.experimental import pallas as pl
from jax.experimental.pallas import tpu as pltpu
from jax.sharding import PartitionSpec as P

H = 8
L = 2
F32 = jnp.float32
BF16 = jnp.bfloat16
EPS = 1e-05
MIB = 1024 * 1024


def split(a):
    if isinstance(a, tuple):
        return a
    hi = a.astype(BF16)
    return hi, (a - hi.astype(F32)).astype(BF16)


def exact(a):
    return (a.astype(BF16),)


def raw(a, b, ca, cb):
    return lax.dot_general(a, b, (((ca,), (cb,)), ((), ())), preferred_element_type=F32)


def product(a, b, ca, cb):
    a, b = split(a), split(b)
    out = raw(a[0], b[0], ca, cb)
    if len(b) > 1:
        out = out + raw(a[0], b[1], ca, cb)
    if len(a) > 1:
        out = out + raw(a[1], b[0], ca, cb)
    return out


def nn(a, b):
    return product(a, b, 1, 0)


def nt(a, b):
    return product(a, b, 1, 1)


def tn(a, b):
    return product(a, b, 0, 0)


def same_head(rows, row_head, cols, col_head):
    r = lax.broadcasted_iota(jnp.int32, (rows, cols), 0) // row_head
    c = lax.broadcasted_iota(jnp.int32, (rows, cols), 1) // col_head
    return r == c


def ones_block(rows, row_head, cols, col_head):
    return exact(same_head(rows, row_head, cols, col_head).astype(F32))


def expand(small, col_head):
    r, cols = small.shape
    tiled = jnp.concatenate([small] * H, axis=0)
    return jnp.where(same_head(H * r, r, cols, col_head), tiled, 0.0)


def fold(dense, col_head):
    rows, cols = dense.shape
    r = rows // H
    head = lax.broadcasted_iota(jnp.int32, (r, cols), 1) // col_head
    out = jnp.where(head == 0, dense[:r], 0.0)
    for h in range(1, H):
        out = jnp.where(head == h, dense[h * r : (h + 1) * r], out)
    return out


def tile_lanes(a, times):
    return jnp.concatenate([a] * times, axis=1)


def norm(field):
    centered = field - jnp.mean(field, axis=-1, keepdims=True)
    rstd = lax.rsqrt(jnp.mean(centered * centered, axis=-1, keepdims=True) + EPS)
    return centered * rstd, rstd


def norm_back(dy, y, rstd):
    return rstd * (
        dy - jnp.mean(dy, axis=-1, keepdims=True) - y * jnp.mean(dy * y, axis=-1, keepdims=True)
    )


def softplus(t):
    return jnp.maximum(t, 0.0) + jnp.log(1.0 + jnp.exp(-jnp.abs(t)))


def front(field, w_in, w_temp, w_slice, live):
    n, width = field.shape
    dh, m = w_slice.shape
    hm = H * m
    nf, rstd = norm(field)
    proj = nn(nf, w_in)
    x, v = proj[:, :width], proj[:, width:]
    wt = tile_lanes(w_temp, H)
    xt = split(x * wt)
    t_wide = nn(xt, ones_block(width, dh, hm, m))
    t_slim = nn(xt, ones_block(width, dh, width, dh))
    r = 1.0 / (0.5 + softplus(t_wide))
    rs = jax.nn.sigmoid(t_slim) / (0.5 + softplus(t_slim))
    logits = nn(x, expand(tile_lanes(w_slice, H), m)) * r
    e = jnp.exp(logits)
    z = nn(e, ones_block(hm, m, hm, m))
    rows = lax.broadcasted_iota(jnp.int32, (n, hm), 0)
    s = jnp.where(rows < live, e / z, 0.0)
    numer = fold(tn(v, s), m)
    denom = jnp.sum(s, axis=0, keepdims=True)
    packed = jnp.concatenate([numer, jnp.broadcast_to(denom, (8, hm))], axis=0)
    return packed, s, proj, nf, rstd, logits, r, rs


def tokens_of(packed, dh):
    inv = 1.0 / (packed[dh : dh + 1] + EPS)
    return packed[:dh] * inv, inv


def middle(packed, w_qkv):
    dh = w_qkv.shape[0]
    tok, inv = tokens_of(packed, dh)
    qkv = tn(w_qkv, tok)
    q, k, v = qkv[:dh], qkv[dh : 2 * dh], qkv[2 * dh :]
    hm = tok.shape[1]
    m = hm // H
    pair = 2 * m
    own = same_head(pair, m, pair, m)
    scale = 1.0 / float(dh) ** 0.5
    maps, mixed = [], []
    for g in range(H // 2):
        lanes = slice(g * pair, (g + 1) * pair)
        e = jnp.where(own, jnp.exp(tn(k[:, lanes], q[:, lanes]) * scale), 0.0)
        a = e / jnp.sum(e, axis=0, keepdims=True)
        maps.append(a)
        mixed.append(nn(v[:, lanes], a))
    return tok, inv, q, k, v, maps, jnp.concatenate(mixed, axis=1)


def middle_back(packed, w_qkv, d_mixed):
    dh = w_qkv.shape[0]
    tok, inv, q, k, v, maps, _ = middle(packed, w_qkv)
    hm = tok.shape[1]
    pair = 2 * (hm // H)
    scale = 1.0 / float(dh) ** 0.5
    dq, dk, dv = [], [], []
    for g in range(H // 2):
        lanes = slice(g * pair, (g + 1) * pair)
        a, dm = maps[g], d_mixed[:, lanes]
        dv.append(nt(dm, a))
        da = tn(v[:, lanes], dm)
        ds = a * (da - jnp.sum(a * da, axis=0, keepdims=True)) * scale
        dk.append(nt(q[:, lanes], ds))
        dq.append(nn(k[:, lanes], ds))
    d_qkv = jnp.concatenate([jnp.concatenate(p, axis=1) for p in (dq, dk, dv)], axis=0)
    g_qkv = nt(tok, d_qkv)
    d_tok = nn(w_qkv, d_qkv)
    d_numer = d_tok * inv
    d_denom = -jnp.sum(d_tok * tok, axis=0, keepdims=True) * inv
    return g_qkv, d_numer, d_denom


def front_back(ds, d_numer, d_denom, s, proj, nf, logits, r, rs, w_in, w_temp, w_slice):
    width = proj.shape[1] // 2
    dh, m = w_slice.shape
    hm = H * m
    x, v = proj[:, :width], proj[:, width:]
    d_blk = split(expand(d_numer, m))
    ds = ds + nn(v, d_blk) + d_denom
    dv = nt(s, d_blk)
    sds = s * ds
    d_logits = sds - s * nn(sds, ones_block(hm, m, hm, m))
    d_t = -rs * nn(d_logits * logits, ones_block(hm, m, width, dh))
    du = split(d_logits * r)
    wt = tile_lanes(w_temp, H)
    dx = nt(du, expand(tile_lanes(w_slice, H), m)) + d_t * wt
    g_temp = jnp.sum(x * d_t, axis=0, keepdims=True)
    g_slice = fold(tn(x, du), m)
    g_slice = sum(g_slice[:, g * 2 * m : (g + 1) * 2 * m] for g in range(H // 2))
    g_slice = g_slice[:, :m] + g_slice[:, m:]
    d_proj = split(jnp.concatenate([dx, dv], axis=1))
    g_in = tn(nf, d_proj)
    return d_proj, g_in, g_temp, g_slice


def gelu_parts(pre):
    c = 0.7978845608028654
    sq = pre * pre
    t = jnp.tanh(c * pre * (1.0 + 0.044715 * sq))
    hid = 0.5 * pre * (1.0 + t)
    slope = 0.5 * (1.0 + t) + 0.5 * pre * (1.0 - t * t) * c * (1.0 + 3 * 0.044715 * sq)
    return hid, slope


def rear(field, s, mixed, w_out, w_up, w_down):
    m = mixed.shape[1] // H
    des = nt(s, expand(mixed, m))
    first = field + nn(des, w_out)
    n1, rstd1 = norm(first)
    pre = nn(n1, w_up)
    hid, _ = gelu_parts(pre)
    return first + nn(hid, w_down), des, n1, rstd1, pre


def rear_back(g, s, mixed, des, n1, rstd1, pre, w_out, w_up, w_down):
    m = mixed.shape[1] // H
    hid, slope = gelu_parts(pre)
    gs = split(g)
    g_down = tn(hid, gs)
    d_pre = split(nt(gs, w_down) * slope)
    g_up = tn(n1, d_pre)
    d_first = g + norm_back(nt(d_pre, w_up), n1, rstd1)
    dfs = split(d_first)
    g_out = tn(des, dfs)
    d_des = split(nt(dfs, w_out))
    ds = nn(d_des, expand(mixed, m))
    d_mixed = fold(tn(d_des, s), m)
    return d_first, ds, d_mixed, g_out, g_up, g_down


def aligned(rows):
    return -(-rows // 8) * 8


def slabs(value):
    return [value[:, i : i + 256] for i in range(0, value.shape[1], 256)]


def scatter(count, pieces, keep, send):
    me = lax.axis_index("cell")
    core = lax.rem(me, 2)

    def put(mine, other):
        for c in range(count):
            slot = (c ^ me) // 2
            at = 0
            for piece in pieces:
                rows = sum(p.shape[0] for p in piece) // count
                which, start = divmod(c * rows, piece[0].shape[0])
                ref = mine if c % 2 == 0 else other
                ref[slot, at : at + rows] = piece[which][start : start + rows]
                at += aligned(rows)

    pl.when(core == 0)(lambda: put(keep, send))
    pl.when(core == 1)(lambda: put(send, keep))


def gather(count, own, other, pieces):
    me = lax.axis_index("cell")
    core = lax.rem(me, 2)

    def take(mine, theirs):
        for c in range(count):
            slot = (c ^ me) // 2
            at = 0
            for rows, targets in pieces:
                each = rows // count
                which, start = divmod(c * each, rows // len(targets))
                src = mine if c % 2 == 0 else theirs
                targets[which](start, src[slot, at : at + each])
                at += aligned(each)

    pl.when(core == 0)(lambda: take(own, other))
    pl.when(core == 1)(lambda: take(other, own))


def into(ref, layer, column, base=0):
    def write(start, value):
        start = base + start
        ref[layer, start : start + value.shape[0], column : column + 256] = value

    return write


def rows_of(ref):
    def write(start, value):
        ref[start : start + value.shape[0]] = value

    return write


def store(refs, values):
    for ref, value in zip(refs, values, strict=True):
        ref[...] = value


def pack_small(g_temp, g_slice, g_head, hm):
    dh, m = g_slice.shape
    width = g_temp.shape[1]
    left = jnp.concatenate([g_temp, g_head, jnp.zeros((8 - 3, width), F32)], axis=0)
    run = dh // 8
    right = jnp.concatenate([g_slice[i * 8 : i * 8 + 8] for i in range(run)], axis=1)
    return left, right


def kernel_a(live, field, w_in, w_temp, w_slice, *out):
    store(out, front(field[...], w_in[...], w_temp[0:1], w_slice[...], live[0]))


def kernel_b(live, pa, pb, field, s, w_qkv, w_out, w_up, w_down, w_in, w_temp, w_slice, *out):
    mixed = middle(pa[...] + pb[...], w_qkv[...])[-1]
    f1, des, n1, rstd1, pre = rear(field[...], s[...], mixed, w_out[...], w_up[...], w_down[...])
    store(out[:5], (mixed, des, n1, rstd1, pre))
    out[5][...] = f1
    store(out[6:], front(f1, w_in[...], w_temp[1:2], w_slice[...], live[0]))


def kernel_c(count, live, pa, pb, field, s, w_qkv, w_out, w_up, w_down, w_head, cot, *out):
    pred, g_head, d_first, ds, d_mixed, keep, send = out
    n, width = field.shape
    mixed = middle(pa[...] + pb[...], w_qkv[...])[-1]
    s = s[...]
    f2, des, n1, rstd1, pre = rear(field[...], s, mixed, w_out[...], w_up[...], w_down[...])
    n2, rstd2 = norm(f2)
    wh = jnp.concatenate([w_head[...], jnp.zeros((6, width), F32)], axis=0)
    n2s = split(n2)
    pred[...] = nt(wh, n2s)[:2]
    lanes = lax.broadcasted_iota(jnp.int32, cot.shape, 1)
    dp = jnp.where(lanes < live[0], cot[...], 0.0)
    dp = jnp.concatenate([dp, jnp.zeros((6, n), F32)], axis=0)
    g_head[...] = nn(dp, n2s)
    g = norm_back(tn(dp, wh), n2, rstd2)
    d_first[...], ds[...], d_mixed[...], g_out, g_up, g_down = rear_back(
        g, s, mixed, des, n1, rstd1, pre, w_out[...], w_up[...], w_down[...]
    )
    halves = [g_out[: width // 2], g_out[width // 2 :]]
    scatter(count, [[g_down], [halves[0]], slabs(g_up), [halves[1]]], keep, send)


def kernel_d(
    count, pa, pb, ma, mb, w_qkv, g_head, d_first, ds, s, proj, nf, rstd, logits, r, rs,
    w_in, w_temp, w_slice, s0, mixed0, des0, n10, rstd10, pre0, w_out0, w_up0, w_down0,
    g_qkv, ds0, d_mixed0, keep, send,
):
    width = nf.shape[1]
    g_qkv[...], d_numer, d_denom = middle_back(pa[...] + pb[...], w_qkv[...], ma[...] + mb[...])
    d_proj, g_in, g_temp, g_slice = front_back(
        ds[...], d_numer, d_denom, s[...], proj[...], nf[...], logits[...], r[...], rs[...],
        w_in[...], w_temp[1:2], w_slice[...],
    )
    g = d_first[...] + norm_back(nt(d_proj, w_in[...]), nf[...], rstd[...])
    _, ds0[...], d_mixed, g_out, g_up, g_down = rear_back(
        g, s0[...], mixed0[...], des0[...], n10[...], rstd10[...], pre0[...],
        w_out0[...], w_up0[...], w_down0[...],
    )
    left, right = pack_small(g_temp, g_slice, g_head[:2], None)
    d_mixed0[...] = jnp.concatenate([d_mixed, jnp.concatenate([left, right], axis=1)], axis=0)
    halves = [g_out[: width // 2], g_out[width // 2 :]]
    ins = slabs(g_in)
    scatter(
        count, [[g_down], [halves[0]], [ins[0]], slabs(g_up), [halves[1]], [ins[1]]], keep, send
    )


def kernel_e(
    count, pa, pb, ma, mb, w_qkv, ds, s, proj, nf, logits, r, rs, w_in, w_temp, w_slice,
    g_qkv, small, keep, send,
):
    dh = w_qkv.shape[0]
    dm = ma[...] + mb[...]
    small[...] = dm[dh:]
    g_qkv[...], d_numer, d_denom = middle_back(pa[...] + pb[...], w_qkv[...], dm[:dh])
    _, g_in, g_temp, g_slice = front_back(
        ds[...], d_numer, d_denom, s[...], proj[...], nf[...], logits[...], r[...], rs[...],
        w_in[...], w_temp[0:1], w_slice[...],
    )
    left, right = pack_small(g_temp, g_slice, jnp.zeros((2, g_temp.shape[1]), F32), None)
    rest = jnp.zeros((8 * count - 16, g_temp.shape[1]), F32)
    ins = slabs(g_in)
    scatter(
        count, [[ins[0]], [jnp.concatenate([left, right, rest], axis=0)], [ins[1]]], keep, send
    )


def kernel_f(
    count, own1, oth1, own2, oth2, own3, oth3, gq0, gq1, small1,
    g_in, g_temp, g_slice, g_qkv, g_out, g_up, g_down, g_head, small0,
):
    width = g_out.shape[1]
    dh, m = g_slice.shape[1:]
    ff = g_up.shape[2]

    def down(l):
        return ff, [into(g_down, l, 0)]

    def up(l):
        return width * (ff // 256), [into(g_up, l, i) for i in range(0, ff, 256)]

    def out(l, part):
        return width // 2, [into(g_out, l, 0, part * (width // 2))]

    def ins(l, part):
        return width, [into(g_in, l, part * width)]

    gather(count, own1, oth1, [down(1), out(1, 0), up(1), out(1, 1)])
    gather(count, own2, oth2, [down(0), out(0, 0), ins(1, 0), up(0), out(0, 1), ins(1, 1)])
    gather(count, own3, oth3, [ins(0, 0), (8 * count, [rows_of(small0)]), ins(0, 1)])
    g_qkv[0] = gq0[...]
    g_qkv[1] = gq1[...]
    for l, (left, right) in enumerate(
        ((small0[:8], small0[8:16]), (small1[:, :width], small1[:, width:]))
    ):
        g_temp[l : l + 1] = sum(left[:1, h * dh : (h + 1) * dh] for h in range(H))
        for i in range(dh // 8):
            g_slice[l, i * 8 : i * 8 + 8] = right[:, i * m : (i + 1) * m]
    g_head[...] = small1[1:3, :width]


VM = pl.BlockSpec(memory_space=pltpu.VMEM)
SM = pl.BlockSpec(memory_space=pltpu.SMEM)
HBM = pl.BlockSpec(memory_space=pltpu.HBM)


class Fetched:
    def __init__(self, source, target, sem):
        self.copy = pltpu.make_async_copy(source, target, sem)
        self.copy.start()
        self.target, self.waiting = target, True
        self.shape = target.shape

    def finish(self):
        if self.waiting:
            self.copy.wait()
            self.waiting = False

    def __getitem__(self, index):
        self.finish()
        return self.target[index]


class Emitted:
    def __init__(self, source, target, sem):
        self.copy = pltpu.make_async_copy(source, target, sem)
        self.source, self.started = source, False
        self.shape = source.shape

    def __setitem__(self, index, value):
        self.source[index] = value
        if index is Ellipsis:
            self.start()

    def start(self):
        self.copy.start()
        self.started = True

    def finish(self):
        if not self.started:
            self.copy.start()
        self.copy.wait()


class Far:
    def __init__(self, what, layer=None):
        self.what, self.layer = what, layer


def call(body, shapes, *args, name, scratch=(), flops=2e9, vmem=24, final=False):
    specs, arrays, held, far_in, far_out, out_specs, out_shapes = [], [], [], [], [], [], []
    for a in args:
        if isinstance(a, Far):
            far_in.append((len(arrays), a.layer))
            held.append(pltpu.VMEM(a.what.shape if a.layer is None else a.what.shape[1:], F32))
            specs.append(HBM)
            a = pltpu.with_memory_space_constraint(a.what, pltpu.HBM)
        else:
            specs.append(SM if a.dtype == jnp.int32 else VM)
            if a.dtype != jnp.int32:
                a = pltpu.with_memory_space_constraint(a, pltpu.VMEM)
        arrays.append(a)
    for s in shapes:
        if isinstance(s, Far):
            far_out.append(len(arrays) + len(out_shapes))
            held.append(pltpu.VMEM(s.what, F32))
            s = s.what
            out_specs.append(HBM)
            out_shapes.append(pltpu.HBM(s, F32))
        else:
            out_specs.append(VM)
            out_shapes.append(jax.ShapeDtypeStruct(s, F32) if final else pltpu.VMEM(s, F32))
    count = len(arrays) + len(shapes)
    copies = len(held)

    def whole(*refs):
        own, extra = list(refs[:count]), refs[count:]
        moved = []
        for at, layer in far_in:
            i = len(moved)
            source = own[at] if layer is None else own[at].at[layer]
            own[at] = Fetched(source, extra[i], extra[copies].at[i])
            moved.append(own[at])
        for at in far_out:
            i = len(moved)
            own[at] = Emitted(extra[i], own[at], extra[copies].at[i])
            moved.append(own[at])
        body(*own, *extra[copies + bool(copies) :])
        for m in moved:
            m.finish()

    if held:
        held.append(pltpu.SemaphoreType.DMA((copies,)))
    return pl.pallas_call(
        whole,
        out_shape=out_shapes,
        in_specs=specs,
        out_specs=out_specs,
        scratch_shapes=held + list(scratch),
        compiler_params=pltpu.CompilerParams(vmem_limit_bytes=vmem * MIB),
        cost_estimate=pl.CostEstimate(
            flops=int(flops), bytes_accessed=int(flops / 100), transcendentals=0
        ),
        name=name,
    )(*arrays)


def swap(a, bit, count):
    return lax.ppermute(a, "cell", [(i, i ^ bit) for i in range(count)])


def masks_of(group):
    masks = [0]
    for bit in group:
        masks += [m | bit for m in masks]
    return masks


def pairs(count):
    bits = [1 << i for i in range(1, count.bit_length() - 1)]
    return [tuple(bits[i : i + 2]) for i in range(0, len(bits), 2)]


class Small:
    def __init__(self, a, count):
        self.a, self.count = a, count
        self.groups = [(1,)] + pairs(count)

    def launch(self):
        self.come = [swap(self.a, m, self.count) for m in masks_of(self.groups[0])[1:]]

    def job(self):
        def add(a, *come):
            if len(come) == 1:
                return [a + come[0]]
            return [(a + come[0]) + (come[1] + come[2])]

        return add, [self.a, *self.come]

    def take(self, values):
        (self.a,) = values
        self.groups = self.groups[1:]

    @property
    def last(self):
        return len(self.groups) == 1

    def parts(self):
        if len(self.come) == 1:
            return self.a, self.come[0]
        return self.a + self.come[0], self.come[1] + self.come[2]


class Chunks:
    def __init__(self, keep, send, a_rows, count):
        self.count = count
        rows = keep.shape[1]
        groups = pairs(count)
        bits = sorted((b for g in groups for b in g), reverse=True)
        if a_rows is None:
            self.sizes, plans = [rows], [groups]
        else:
            self.sizes = [a_rows, rows - a_rows]
            plans = [[(b,) for g in groups for b in g], [(b,) for g in groups for b in g[::-1]]]
        self.stages = list(zip(*plans))
        self.at, self.phase = 0, "core"
        self.have, self.sends = [keep], [[(send, 1)]]
        self.left = [list(bits) for _ in self.sizes]
        self.bits = bits

    def launch(self):
        self.come = [[swap(a, m, self.count) for a, m in sends] for sends in self.sends]

    @property
    def done(self):
        return self.phase == "done"

    def job(self):
        sizes, left, phase, at, stages = self.sizes, self.left, self.phase, self.at, self.stages
        shapes = [len(c) for c in self.come]
        flat = [x for h, c in zip(self.have, self.come) for x in (h, *c)]

        def unflatten(flat):
            flat, out = list(flat), []
            for k in shapes:
                out.append((flat[0], flat[1 : k + 1]))
                flat = flat[k + 1 :]
            return out

        def rows_split(parts):
            if len(parts) == len(sizes):
                return parts
            a = sizes[0]
            return [parts[0][..., :a, :], parts[0][..., a:, :]]

        def cut(parts, stage):
            out = []
            same = len(parts) == 2 and stage[0] == stage[1]
            if same:
                parts = [jnp.concatenate(parts, axis=-2)]
            for p, l, group in zip(parts, left, stage):
                for mask in masks_of(group):
                    piece, rest = p, list(l)
                    for bit in group:
                        axis = rest.index(bit)
                        piece = lax.index_in_dim(piece, int(mask & bit > 0), axis, keepdims=False)
                        rest.remove(bit)
                    out.append(piece)
            return out

        def summed(flat):
            out = []
            for h, c in unflatten(flat):
                for x in c:
                    h = h + x
                out.append(h)
            return out

        def reduce(*flat):
            parts = summed(flat)
            if phase == "core":
                parts = [parts[0].reshape((2,) * len(left[0]) + parts[0].shape[1:])]
                parts = rows_split(parts)
            if at < len(stages):
                return cut(parts, stages[at])
            return parts

        def gather_one(*flat):
            out = []
            stage = stages[at]
            for (h, c), l, group in zip(unflatten(flat), left, stage):
                done = list(l)
                pieces = dict(zip(masks_of(group), (h, *c)))
                for bit in reversed(group):
                    done = sorted(done + [bit], reverse=True)
                    axis = done.index(bit)
                    pieces = {
                        m: jnp.stack([v, pieces[m | bit]], axis=axis)
                        for m, v in pieces.items()
                        if not m & bit
                    }
                out.append(pieces[0])
            if at == 0:
                if len(out) == 2:
                    out = [jnp.concatenate(out, axis=-2)]
                return [out[0].reshape((-1,) + out[0].shape[-2:])]
            before = stages[at - 1]
            if len(out) == 1 and len(sizes) == 2 and before[0] != before[1]:
                out = rows_split(out)
            return out

        return (gather_one if phase == "gather" else reduce), flat

    def take(self, values):
        values = list(values)
        if self.phase in ("core", "reduce"):
            if self.at < len(self.stages):
                stage = self.stages[self.at]
                self.have, self.sends = [], []
                same = len(stage) == 2 and stage[0] == stage[1]
                for group in stage[:1] if same else stage:
                    masks = masks_of(group)
                    self.have.append(values[0])
                    self.sends.append(list(zip(values[1 : len(masks)], masks[1:])))
                    values = values[len(masks) :]
                self.left = [[b for b in l if b not in g] for l, g in zip(self.left, stage)]
                self.at += 1
                self.phase = "reduce"
                return
            self.phase = "gather"
            self.at -= 1
        else:
            stage = self.stages[self.at]
            self.left = [sorted(l + list(g), reverse=True) for l, g in zip(self.left, stage)]
            self.at -= 1
        self.have = values
        if self.at < 0:
            self.phase = "last"
            self.sends = [[(values[0], 1)]]
        else:
            stage = self.stages[self.at]
            self.sends = [
                [(v, m) for m in masks_of(g)[1:]] for v, g in zip(values, stage)
            ]

    def result(self):
        return self.have[0], self.come[0][0]


def step(*works, name):
    jobs = [w.job() for w in works]
    outs = [jax.eval_shape(lambda *a, fn=fn: fn(*a), *arrays) for fn, arrays in jobs]

    def body(*refs):
        refs = list(refs)
        ins, results = refs[: sum(len(a) for _, a in jobs)], refs[sum(len(a) for _, a in jobs) :]
        for fn, arrays in jobs:
            values = fn(*[r[...] for r in ins[: len(arrays)]])
            ins = ins[len(arrays) :]
            store(results[: len(values)], values)
            results = results[len(values) :]

    values = call(
        body, [o.shape for out in outs for o in out], *[a for _, arrays in jobs for a in arrays],
        name=name, flops=1e8, vmem=12,
    )
    for w, out in zip(works, outs):
        w.take(values[: len(out)])
        values = values[len(out) :]


def sum_small(a, count):
    small = Small(a, count)
    small.launch()
    while not small.last:
        step(small, name="add")
        small.launch()
    return small.parts()


def shards(
    count,
    features,
    counts,
    cotangent,
    weight_in,
    weight_temp,
    weight_slice,
    weight_qkv,
    weight_out,
    expansion_matrix,
    weight_down,
    weight_head,
):
    n, width = features.shape
    dh, m = weight_slice.shape[1:]
    ff = expansion_matrix.shape[2]
    hm = H * m
    far = lambda *arrays: [Far(a) for a in arrays]
    qkv = lambda l: Far(weight_qkv, l)
    rear_w = lambda l: [Far(w, l) for w in (weight_out, expansion_matrix, weight_down)]
    front_w = lambda l: [Far(weight_in, l), Far(weight_temp), Far(weight_slice, l)]

    kept = [(n, hm), (n, 2 * width), (n, width), (n, 1), (n, hm), (n, hm), (n, width)]
    front_shapes = [(dh + 8, hm)] + [Far(s) for s in kept]
    rear_shapes = [Far(s) for s in [(dh, hm), (n, width), (n, width), (n, 1), (n, ff)]]
    run = lambda *rows: sum(aligned(r // count) for r in rows)
    a1 = run(ff, width // 2)
    a2 = run(ff, width // 2, width)
    a3 = run(width, 8 * count, width)
    chunks = lambda rows: [(count // 2, rows, 256)] * 2
    with_count = lambda body: partial(body, count)

    p0, s0, proj0, nf0, _, lg0, r0, rs0 = call(
        kernel_a, front_shapes, counts, Far(features), *front_w(0), name="front0"
    )
    p0 = sum_small(p0, count)
    mix0, des0, n10, rd10, pre0, f1, p1, s1, proj1, nf1, rstd1, lg1, r1, rs1 = call(
        kernel_b, rear_shapes + [Far((n, width))] + front_shapes,
        counts, *p0, Far(features), Far(s0), qkv(0), *rear_w(0), *front_w(1), name="rear0_front1",
    )
    p1 = sum_small(p1, count)
    pred, g_head, d_first, ds1, dm, keep, send = call(
        with_count(kernel_c),
        [Far((2, n)), (8, width), (n, width), (n, hm), (dh, hm)] + chunks(2 * a1),
        counts, *p1, Far(f1), Far(s1), qkv(1), *rear_w(1), Far(weight_head.T), Far(cotangent),
        name="rear1_head_back1",
    )

    dm = Small(dm, count)
    first = Chunks(keep, send, a1, count)
    dm.launch()
    first.launch()
    step(dm, name="add")
    while not dm.last:
        dm.launch()
        step(dm, first, name="add_chunks")
        first.launch()
    dm.launch()

    gq1, ds0, dm0, keep, send = call(
        with_count(kernel_d), [(dh, 3 * dh), (n, hm), (dh + 8, hm)] + chunks(2 * a2),
        *p1, *dm.parts(), qkv(1), g_head, d_first, ds1, *far(s1, proj1, nf1, rstd1, lg1, r1, rs1),
        *front_w(1), *far(s0, mix0, des0, n10, rd10, pre0), *rear_w(0), name="back_front1_rear0",
    )

    dm = Small(dm0, count)
    second = Chunks(keep, send, a2, count)
    dm.launch()
    second.launch()
    while not dm.last:
        step(dm, first, second, name="add_chunks")
        dm.launch()
        first.launch()
        second.launch()

    gq0, small1, keep, send = call(
        with_count(kernel_e), [(dh, 3 * dh), (8, hm)] + chunks(a3),
        *p0, *dm.parts(), qkv(0), ds0, *far(s0, proj0, nf0, lg0, r0, rs0), *front_w(0),
        name="back_front0",
    )
    third = Chunks(keep, send, None, count)
    third.launch()
    works = [first, second, third]
    while True:
        busy = [w for w in works if w.phase != "last"]
        if not busy:
            break
        step(*busy, name="chunks")
        for w in busy:
            w.launch()

    *grads, g_head = call(
        with_count(kernel_f),
        [
            (L, width, 2 * width), (L, dh), (L, dh, m), (L, dh, 3 * dh), (L, width, width),
            (L, width, ff), (L, ff, width), (2, width),
        ],
        *first.result(), *second.result(), *third.result(), gq0, gq1, small1,
        name="place_gradients", scratch=[pltpu.VMEM((8 * count, 256), F32)], final=True,
    )
    return (pred, *grads, g_head.T)


def solution(mesh):
    cells = P(("grp", "cell"))
    return jax.shard_map(
        partial(shards, mesh.shape["cell"]),
        mesh=mesh,
        in_specs=(P(("grp", "cell"), None), cells, P(None, ("grp", "cell"))) + (P(),) * 8,
        out_specs=(
            P(None, ("grp", "cell")),
            P("grp", None, None),
            P("grp", None),
            P("grp", None, None),
            P("grp", None, None),
            P("grp", None, None),
            P("grp", None, None),
            P("grp", None, None),
            P("grp", None),
        ),
        check_vma=False,
    )
```

```python
from functools import partial

import jax
import jax.numpy as jnp
from jax import lax
from jax.experimental import pallas as pl
from jax.experimental.pallas import tpu as pltpu
from jax.sharding import PartitionSpec as P

H = 8
L = 2
F32 = jnp.float32
BF16 = jnp.bfloat16
EPS = 1e-05
MIB = 1024 * 1024


def split(a):
    if isinstance(a, tuple):
        return a
    hi = a.astype(BF16)
    return hi, (a - hi.astype(F32)).astype(BF16)


def exact(a):
    return (a.astype(BF16),)


def raw(a, b, ca, cb):
    return lax.dot_general(a, b, (((ca,), (cb,)), ((), ())), preferred_element_type=F32)


def product(a, b, ca, cb):
    a, b = split(a), split(b)
    out = raw(a[0], b[0], ca, cb)
    if len(b) > 1:
        out = out + raw(a[0], b[1], ca, cb)
    if len(a) > 1:
        out = out + raw(a[1], b[0], ca, cb)
    return out


def nn(a, b):
    return product(a, b, 1, 0)


def nt(a, b):
    return product(a, b, 1, 1)


def tn(a, b):
    return product(a, b, 0, 0)


def same_head(rows, row_head, cols, col_head):
    r = lax.broadcasted_iota(jnp.int32, (rows, cols), 0) // row_head
    c = lax.broadcasted_iota(jnp.int32, (rows, cols), 1) // col_head
    return r == c


def ones_block(rows, row_head, cols, col_head):
    return exact(same_head(rows, row_head, cols, col_head).astype(F32))


def expand(small, col_head):
    r, cols = small.shape
    tiled = jnp.concatenate([small] * H, axis=0)
    return jnp.where(same_head(H * r, r, cols, col_head), tiled, 0.0)


def fold(dense, col_head):
    rows, cols = dense.shape
    r = rows // H
    head = lax.broadcasted_iota(jnp.int32, (r, cols), 1) // col_head
    out = jnp.where(head == 0, dense[:r], 0.0)
    for h in range(1, H):
        out = jnp.where(head == h, dense[h * r : (h + 1) * r], out)
    return out


def tile_lanes(a, times):
    return jnp.concatenate([a] * times, axis=1)


def norm(field):
    centered = field - jnp.mean(field, axis=-1, keepdims=True)
    rstd = lax.rsqrt(jnp.mean(centered * centered, axis=-1, keepdims=True) + EPS)
    return centered * rstd, rstd


def norm_back(dy, y, rstd):
    return rstd * (
        dy - jnp.mean(dy, axis=-1, keepdims=True) - y * jnp.mean(dy * y, axis=-1, keepdims=True)
    )


def softplus(t):
    return jnp.maximum(t, 0.0) + jnp.log(1.0 + jnp.exp(-jnp.abs(t)))


def front(field, w_in, w_temp, w_slice, live):
    n, width = field.shape
    dh, m = w_slice.shape
    hm = H * m
    nf, rstd = norm(field)
    proj = nn(nf, w_in)
    x, v = proj[:, :width], proj[:, width:]
    wt = tile_lanes(w_temp, H)
    xt = split(x * wt)
    t_wide = nn(xt, ones_block(width, dh, hm, m))
    t_slim = nn(xt, ones_block(width, dh, width, dh))
    r = 1.0 / (0.5 + softplus(t_wide))
    rs = jax.nn.sigmoid(t_slim) / (0.5 + softplus(t_slim))
    logits = nn(x, expand(tile_lanes(w_slice, H), m)) * r
    e = jnp.exp(logits)
    z = nn(e, ones_block(hm, m, hm, m))
    rows = lax.broadcasted_iota(jnp.int32, (n, hm), 0)
    s = jnp.where(rows < live, e / z, 0.0)
    numer = fold(tn(v, s), m)
    denom = jnp.sum(s, axis=0, keepdims=True)
    packed = jnp.concatenate([numer, jnp.broadcast_to(denom, (8, hm))], axis=0)
    return packed, s, proj, nf, rstd, logits, r, rs


def tokens_of(packed, dh):
    inv = 1.0 / (packed[dh : dh + 1] + EPS)
    return packed[:dh] * inv, inv


def middle(packed, w_qkv):
    dh = w_qkv.shape[0]
    tok, inv = tokens_of(packed, dh)
    qkv = tn(w_qkv, tok)
    q, k, v = qkv[:dh], qkv[dh : 2 * dh], qkv[2 * dh :]
    hm = tok.shape[1]
    m = hm // H
    pair = 2 * m
    own = same_head(pair, m, pair, m)
    scale = 1.0 / float(dh) ** 0.5
    maps, mixed = [], []
    for g in range(H // 2):
        lanes = slice(g * pair, (g + 1) * pair)
        e = jnp.where(own, jnp.exp(tn(k[:, lanes], q[:, lanes]) * scale), 0.0)
        a = e / jnp.sum(e, axis=0, keepdims=True)
        maps.append(a)
        mixed.append(nn(v[:, lanes], a))
    return tok, inv, q, k, v, maps, jnp.concatenate(mixed, axis=1)


def middle_back(packed, w_qkv, d_mixed):
    dh = w_qkv.shape[0]
    tok, inv, q, k, v, maps, _ = middle(packed, w_qkv)
    hm = tok.shape[1]
    pair = 2 * (hm // H)
    scale = 1.0 / float(dh) ** 0.5
    dq, dk, dv = [], [], []
    for g in range(H // 2):
        lanes = slice(g * pair, (g + 1) * pair)
        a, dm = maps[g], d_mixed[:, lanes]
        dv.append(nt(dm, a))
        da = tn(v[:, lanes], dm)
        ds = a * (da - jnp.sum(a * da, axis=0, keepdims=True)) * scale
        dk.append(nt(q[:, lanes], ds))
        dq.append(nn(k[:, lanes], ds))
    d_qkv = jnp.concatenate([jnp.concatenate(p, axis=1) for p in (dq, dk, dv)], axis=0)
    g_qkv = nt(tok, d_qkv)
    d_tok = nn(w_qkv, d_qkv)
    d_numer = d_tok * inv
    d_denom = -jnp.sum(d_tok * tok, axis=0, keepdims=True) * inv
    return g_qkv, d_numer, d_denom


def front_back(ds, d_numer, d_denom, s, proj, nf, logits, r, rs, w_in, w_temp, w_slice):
    width = proj.shape[1] // 2
    dh, m = w_slice.shape
    hm = H * m
    x, v = proj[:, :width], proj[:, width:]
    d_blk = split(expand(d_numer, m))
    ds = ds + nn(v, d_blk) + d_denom
    dv = nt(s, d_blk)
    sds = s * ds
    d_logits = sds - s * nn(sds, ones_block(hm, m, hm, m))
    d_t = -rs * nn(d_logits * logits, ones_block(hm, m, width, dh))
    du = split(d_logits * r)
    wt = tile_lanes(w_temp, H)
    dx = nt(du, expand(tile_lanes(w_slice, H), m)) + d_t * wt
    g_temp = jnp.sum(x * d_t, axis=0, keepdims=True)
    g_slice = fold(tn(x, du), m)
    g_slice = sum(g_slice[:, g * 2 * m : (g + 1) * 2 * m] for g in range(H // 2))
    g_slice = g_slice[:, :m] + g_slice[:, m:]
    d_proj = split(jnp.concatenate([dx, dv], axis=1))
    g_in = tn(nf, d_proj)
    return d_proj, g_in, g_temp, g_slice


def gelu_parts(pre):
    c = 0.7978845608028654
    sq = pre * pre
    t = jnp.tanh(c * pre * (1.0 + 0.044715 * sq))
    hid = 0.5 * pre * (1.0 + t)
    slope = 0.5 * (1.0 + t) + 0.5 * pre * (1.0 - t * t) * c * (1.0 + 3 * 0.044715 * sq)
    return hid, slope


def rear(field, s, mixed, w_out, w_up, w_down):
    m = mixed.shape[1] // H
    des = nt(s, expand(mixed, m))
    first = field + nn(des, w_out)
    n1, rstd1 = norm(first)
    pre = nn(n1, w_up)
    hid, _ = gelu_parts(pre)
    return first + nn(hid, w_down), des, n1, rstd1, pre


def rear_back(g, s, mixed, des, n1, rstd1, pre, w_out, w_up, w_down):
    m = mixed.shape[1] // H
    hid, slope = gelu_parts(pre)
    gs = split(g)
    g_down = tn(hid, gs)
    d_pre = split(nt(gs, w_down) * slope)
    g_up = tn(n1, d_pre)
    d_first = g + norm_back(nt(d_pre, w_up), n1, rstd1)
    dfs = split(d_first)
    g_out = tn(des, dfs)
    d_des = split(nt(dfs, w_out))
    ds = nn(d_des, expand(mixed, m))
    d_mixed = fold(tn(d_des, s), m)
    return d_first, ds, d_mixed, g_out, g_up, g_down


def aligned(rows):
    return -(-rows // 8) * 8


def slabs(value):
    return [value[:, i : i + 256] for i in range(0, value.shape[1], 256)]


def scatter(count, pieces, keep, send):
    me = lax.axis_index("cell")
    core = lax.rem(me, 2)

    def put(mine, other):
        for c in range(count):
            slot = (c ^ me) // 2
            at = 0
            for piece in pieces:
                rows = sum(p.shape[0] for p in piece) // count
                which, start = divmod(c * rows, piece[0].shape[0])
                ref = mine if c % 2 == 0 else other
                ref[slot, at : at + rows] = piece[which][start : start + rows]
                at += aligned(rows)

    pl.when(core == 0)(lambda: put(keep, send))
    pl.when(core == 1)(lambda: put(send, keep))


def gather(count, own, other, pieces):
    me = lax.axis_index("cell")
    core = lax.rem(me, 2)

    def take(mine, theirs):
        for c in range(count):
            slot = (c ^ me) // 2
            at = 0
            for rows, targets in pieces:
                each = rows // count
                which, start = divmod(c * each, rows // len(targets))
                src = mine if c % 2 == 0 else theirs
                targets[which](start, src[slot, at : at + each])
                at += aligned(each)

    pl.when(core == 0)(lambda: take(own, other))
    pl.when(core == 1)(lambda: take(other, own))


def into(ref, layer, column, base=0):
    def write(start, value):
        start = base + start
        ref[layer, start : start + value.shape[0], column : column + 256] = value

    return write


def rows_of(ref):
    def write(start, value):
        ref[start : start + value.shape[0]] = value

    return write


def store(refs, values):
    for ref, value in zip(refs, values, strict=True):
        ref[...] = value


def pack_small(g_temp, g_slice, g_head, hm):
    dh, m = g_slice.shape
    width = g_temp.shape[1]
    left = jnp.concatenate([g_temp, g_head, jnp.zeros((8 - 3, width), F32)], axis=0)
    run = dh // 8
    right = jnp.concatenate([g_slice[i * 8 : i * 8 + 8] for i in range(run)], axis=1)
    return left, right


def kernel_a(live, field, w_in, w_temp, w_slice, *out):
    store(out, front(field[...], w_in[...], w_temp[0:1], w_slice[...], live[0]))


def kernel_b(live, pa, pb, field, s, w_qkv, w_out, w_up, w_down, w_in, w_temp, w_slice, *out):
    mixed = middle(pa[...] + pb[...], w_qkv[...])[-1]
    f1, des, n1, rstd1, pre = rear(field[...], s[...], mixed, w_out[...], w_up[...], w_down[...])
    store(out[:5], (mixed, des, n1, rstd1, pre))
    out[5][...] = f1
    store(out[6:], front(f1, w_in[...], w_temp[1:2], w_slice[...], live[0]))


def kernel_c(count, live, pa, pb, field, s, w_qkv, w_out, w_up, w_down, w_head, cot, *out):
    pred, g_head, d_first, ds, d_mixed, keep, send = out
    n, width = field.shape
    mixed = middle(pa[...] + pb[...], w_qkv[...])[-1]
    s = s[...]
    f2, des, n1, rstd1, pre = rear(field[...], s, mixed, w_out[...], w_up[...], w_down[...])
    n2, rstd2 = norm(f2)
    wh = jnp.concatenate([w_head[...], jnp.zeros((6, width), F32)], axis=0)
    n2s = split(n2)
    pred[...] = nt(wh, n2s)[:2]
    lanes = lax.broadcasted_iota(jnp.int32, cot.shape, 1)
    dp = jnp.where(lanes < live[0], cot[...], 0.0)
    dp = jnp.concatenate([dp, jnp.zeros((6, n), F32)], axis=0)
    g_head[...] = nn(dp, n2s)
    g = norm_back(tn(dp, wh), n2, rstd2)
    d_first[...], ds[...], d_mixed[...], g_out, g_up, g_down = rear_back(
        g, s, mixed, des, n1, rstd1, pre, w_out[...], w_up[...], w_down[...]
    )
    halves = [g_out[: width // 2], g_out[width // 2 :]]
    scatter(count, [[g_down], [halves[0]], slabs(g_up), [halves[1]]], keep, send)


def kernel_d(
    count, pa, pb, ma, mb, w_qkv, g_head, d_first, ds, s, proj, nf, rstd, logits, r, rs,
    w_in, w_temp, w_slice, s0, mixed0, des0, n10, rstd10, pre0, w_out0, w_up0, w_down0,
    g_qkv, ds0, d_mixed0, keep, send,
):
    width = nf.shape[1]
    g_qkv[...], d_numer, d_denom = middle_back(pa[...] + pb[...], w_qkv[...], ma[...] + mb[...])
    d_proj, g_in, g_temp, g_slice = front_back(
        ds[...], d_numer, d_denom, s[...], proj[...], nf[...], logits[...], r[...], rs[...],
        w_in[...], w_temp[1:2], w_slice[...],
    )
    g = d_first[...] + norm_back(nt(d_proj, w_in[...]), nf[...], rstd[...])
    _, ds0[...], d_mixed, g_out, g_up, g_down = rear_back(
        g, s0[...], mixed0[...], des0[...], n10[...], rstd10[...], pre0[...],
        w_out0[...], w_up0[...], w_down0[...],
    )
    left, right = pack_small(g_temp, g_slice, g_head[:2], None)
    d_mixed0[...] = jnp.concatenate([d_mixed, jnp.concatenate([left, right], axis=1)], axis=0)
    halves = [g_out[: width // 2], g_out[width // 2 :]]
    ins = slabs(g_in)
    scatter(
        count, [[g_down], [halves[0]], [ins[0]], slabs(g_up), [halves[1]], [ins[1]]], keep, send
    )


def kernel_e(
    count, pa, pb, ma, mb, w_qkv, ds, s, proj, nf, logits, r, rs, w_in, w_temp, w_slice,
    g_qkv, small, keep, send,
):
    dh = w_qkv.shape[0]
    dm = ma[...] + mb[...]
    small[...] = dm[dh:]
    g_qkv[...], d_numer, d_denom = middle_back(pa[...] + pb[...], w_qkv[...], dm[:dh])
    _, g_in, g_temp, g_slice = front_back(
        ds[...], d_numer, d_denom, s[...], proj[...], nf[...], logits[...], r[...], rs[...],
        w_in[...], w_temp[0:1], w_slice[...],
    )
    left, right = pack_small(g_temp, g_slice, jnp.zeros((2, g_temp.shape[1]), F32), None)
    rest = jnp.zeros((8 * count - 16, g_temp.shape[1]), F32)
    ins = slabs(g_in)
    scatter(
        count, [[ins[0]], [jnp.concatenate([left, right, rest], axis=0)], [ins[1]]], keep, send
    )


def kernel_f(
    count, own1, oth1, own2, oth2, own3, oth3, gq0, gq1, small1,
    g_in, g_temp, g_slice, g_qkv, g_out, g_up, g_down, g_head, small0,
):
    width = g_out.shape[1]
    dh, m = g_slice.shape[1:]
    ff = g_up.shape[2]

    def down(l):
        return ff, [into(g_down, l, 0)]

    def up(l):
        return width * (ff // 256), [into(g_up, l, i) for i in range(0, ff, 256)]

    def out(l, part):
        return width // 2, [into(g_out, l, 0, part * (width // 2))]

    def ins(l, part):
        return width, [into(g_in, l, part * width)]

    gather(count, own1, oth1, [down(1), out(1, 0), up(1), out(1, 1)])
    gather(count, own2, oth2, [down(0), out(0, 0), ins(1, 0), up(0), out(0, 1), ins(1, 1)])
    gather(count, own3, oth3, [ins(0, 0), (8 * count, [rows_of(small0)]), ins(0, 1)])
    g_qkv[0] = gq0[...]
    g_qkv[1] = gq1[...]
    for l, (left, right) in enumerate(
        ((small0[:8], small0[8:16]), (small1[:, :width], small1[:, width:]))
    ):
        g_temp[l : l + 1] = sum(left[:1, h * dh : (h + 1) * dh] for h in range(H))
        for i in range(dh // 8):
            g_slice[l, i * 8 : i * 8 + 8] = right[:, i * m : (i + 1) * m]
    g_head[...] = small1[1:3, :width]


VM = pl.BlockSpec(memory_space=pltpu.VMEM)
SM = pl.BlockSpec(memory_space=pltpu.SMEM)
HBM = pl.BlockSpec(memory_space=pltpu.HBM)


class Fetched:
    def __init__(self, source, target, sem):
        self.copy = pltpu.make_async_copy(source, target, sem)
        self.copy.start()
        self.target, self.waiting = target, True
        self.shape = target.shape

    def finish(self):
        if self.waiting:
            self.copy.wait()
            self.waiting = False

    def __getitem__(self, index):
        self.finish()
        return self.target[index]


class Emitted:
    def __init__(self, source, target, sem):
        self.copy = pltpu.make_async_copy(source, target, sem)
        self.source, self.started = source, False
        self.shape = source.shape

    def __setitem__(self, index, value):
        self.source[index] = value
        if index is Ellipsis:
            self.start()

    def start(self):
        self.copy.start()
        self.started = True

    def finish(self):
        if not self.started:
            self.copy.start()
        self.copy.wait()


class Far:
    def __init__(self, what, layer=None):
        self.what, self.layer = what, layer


class Order:
    def __init__(self):
        self.token = None


def call(body, shapes, *args, name, order=None, scratch=(), flops=1.5e10, vmem=24, final=False):
    specs, arrays, held, far_in, far_out, out_specs, out_shapes = [], [], [], [], [], [], []
    if order is not None:
        inner, tokens = body, int(order.token is not None)
        args = args + (order.token,) * tokens
        used = len(args) - tokens
        shapes = list(shapes) + [(8, 128)]
        results = len(shapes) - 1

        def body(*refs):
            outs = refs[used + tokens :]
            outs[results][...] = jnp.zeros((8, 128), F32)
            inner(*refs[:used], *outs[:results], *outs[results + 1 :])

    for a in args:
        if isinstance(a, Far):
            far_in.append((len(arrays), a.layer))
            held.append(pltpu.VMEM(a.what.shape if a.layer is None else a.what.shape[1:], F32))
            specs.append(HBM)
            a = pltpu.with_memory_space_constraint(a.what, pltpu.HBM)
        else:
            specs.append(SM if a.dtype == jnp.int32 else VM)
            if a.dtype != jnp.int32:
                a = pltpu.with_memory_space_constraint(a, pltpu.VMEM)
        arrays.append(a)
    for s in shapes:
        if isinstance(s, Far):
            far_out.append(len(arrays) + len(out_shapes))
            held.append(pltpu.VMEM(s.what, F32))
            s = s.what
            out_specs.append(HBM)
            out_shapes.append(pltpu.HBM(s, F32))
        else:
            out_specs.append(VM)
            out_shapes.append(jax.ShapeDtypeStruct(s, F32) if final else pltpu.VMEM(s, F32))
    count = len(arrays) + len(shapes)
    copies = len(held)

    def whole(*refs):
        own, extra = list(refs[:count]), refs[count:]
        moved = []
        for at, layer in far_in:
            i = len(moved)
            source = own[at] if layer is None else own[at].at[layer]
            own[at] = Fetched(source, extra[i], extra[copies].at[i])
            moved.append(own[at])
        for at in far_out:
            i = len(moved)
            own[at] = Emitted(extra[i], own[at], extra[copies].at[i])
            moved.append(own[at])
        body(*own, *extra[copies + bool(copies) :])
        for m in moved:
            m.finish()

    if held:
        held.append(pltpu.SemaphoreType.DMA((copies,)))
    values = pl.pallas_call(
        whole,
        out_shape=out_shapes,
        in_specs=specs,
        out_specs=out_specs,
        scratch_shapes=held + list(scratch),
        compiler_params=pltpu.CompilerParams(vmem_limit_bytes=vmem * MIB),
        cost_estimate=pl.CostEstimate(
            flops=int(flops), bytes_accessed=int(flops / 100), transcendentals=0
        ),
        name=name,
    )(*arrays)
    if order is not None:
        order.token = values[-1]
        values = values[:-1]
    return values


def swap(a, bit, count):
    return lax.ppermute(a, "cell", [(i, i ^ bit) for i in range(count)])


def masks_of(group):
    masks = [0]
    for bit in group:
        masks += [m | bit for m in masks]
    return masks


def pairs(count):
    bits = [1 << i for i in range(1, count.bit_length() - 1)]
    return [tuple(bits[i : i + 2]) for i in range(0, len(bits), 2)]


class Small:
    def __init__(self, a, count):
        self.a, self.count = a, count
        self.groups = [(1,)] + pairs(count)

    def launch(self):
        self.come = [swap(self.a, m, self.count) for m in masks_of(self.groups[0])[1:]]

    def job(self):
        def add(a, *come):
            if len(come) == 1:
                return [a + come[0]]
            return [(a + come[0]) + (come[1] + come[2])]

        return add, [self.a, *self.come]

    def take(self, values):
        (self.a,) = values
        self.groups = self.groups[1:]

    @property
    def last(self):
        return len(self.groups) == 1

    def parts(self):
        if len(self.come) == 1:
            return self.a, self.come[0]
        return self.a + self.come[0], self.come[1] + self.come[2]


class Chunks:
    def __init__(self, keep, send, a_rows, count):
        self.count = count
        rows = keep.shape[1]
        groups = pairs(count)
        bits = sorted((b for g in groups for b in g), reverse=True)
        if a_rows is None:
            self.sizes, plans = [rows], [groups]
        else:
            self.sizes = [a_rows, rows - a_rows]
            plans = [[(b,) for g in groups for b in g], [(b,) for g in groups for b in g[::-1]]]
        self.stages = list(zip(*plans))
        self.at, self.phase = 0, "core"
        self.have, self.sends = [keep], [[(send, 1)]]
        self.left = [list(bits) for _ in self.sizes]
        self.bits = bits

    def launch(self):
        self.come = [[swap(a, m, self.count) for a, m in sends] for sends in self.sends]

    @property
    def done(self):
        return self.phase == "done"

    def job(self):
        sizes, left, phase, at, stages = self.sizes, self.left, self.phase, self.at, self.stages
        shapes = [len(c) for c in self.come]
        flat = [x for h, c in zip(self.have, self.come) for x in (h, *c)]

        def unflatten(flat):
            flat, out = list(flat), []
            for k in shapes:
                out.append((flat[0], flat[1 : k + 1]))
                flat = flat[k + 1 :]
            return out

        def rows_split(parts):
            if len(parts) == len(sizes):
                return parts
            a = sizes[0]
            return [parts[0][..., :a, :], parts[0][..., a:, :]]

        def cut(parts, stage):
            out = []
            same = len(parts) == 2 and stage[0] == stage[1]
            if same:
                parts = [jnp.concatenate(parts, axis=-2)]
            for p, l, group in zip(parts, left, stage):
                for mask in masks_of(group):
                    piece, rest = p, list(l)
                    for bit in group:
                        axis = rest.index(bit)
                        piece = lax.index_in_dim(piece, int(mask & bit > 0), axis, keepdims=False)
                        rest.remove(bit)
                    out.append(piece)
            return out

        def summed(flat):
            out = []
            for h, c in unflatten(flat):
                for x in c:
                    h = h + x
                out.append(h)
            return out

        def reduce(*flat):
            parts = summed(flat)
            if phase == "core":
                parts = [parts[0].reshape((2,) * len(left[0]) + parts[0].shape[1:])]
                parts = rows_split(parts)
            if at < len(stages):
                return cut(parts, stages[at])
            return parts

        def gather_one(*flat):
            out = []
            stage = stages[at]
            for (h, c), l, group in zip(unflatten(flat), left, stage):
                done = list(l)
                pieces = dict(zip(masks_of(group), (h, *c)))
                for bit in reversed(group):
                    done = sorted(done + [bit], reverse=True)
                    axis = done.index(bit)
                    pieces = {
                        m: jnp.stack([v, pieces[m | bit]], axis=axis)
                        for m, v in pieces.items()
                        if not m & bit
                    }
                out.append(pieces[0])
            if at == 0:
                if len(out) == 2:
                    out = [jnp.concatenate(out, axis=-2)]
                return [out[0].reshape((-1,) + out[0].shape[-2:])]
            before = stages[at - 1]
            if len(out) == 1 and len(sizes) == 2 and before[0] != before[1]:
                out = rows_split(out)
            return out

        return (gather_one if phase == "gather" else reduce), flat

    def take(self, values):
        values = list(values)
        if self.phase in ("core", "reduce"):
            if self.at < len(self.stages):
                stage = self.stages[self.at]
                self.have, self.sends = [], []
                same = len(stage) == 2 and stage[0] == stage[1]
                for group in stage[:1] if same else stage:
                    masks = masks_of(group)
                    self.have.append(values[0])
                    self.sends.append(list(zip(values[1 : len(masks)], masks[1:])))
                    values = values[len(masks) :]
                self.left = [[b for b in l if b not in g] for l, g in zip(self.left, stage)]
                self.at += 1
                self.phase = "reduce"
                return
            self.phase = "gather"
            self.at -= 1
        else:
            stage = self.stages[self.at]
            self.left = [sorted(l + list(g), reverse=True) for l, g in zip(self.left, stage)]
            self.at -= 1
        self.have = values
        if self.at < 0:
            self.phase = "last"
            self.sends = [[(values[0], 1)]]
        else:
            stage = self.stages[self.at]
            self.sends = [
                [(v, m) for m in masks_of(g)[1:]] for v, g in zip(values, stage)
            ]

    def result(self):
        return self.have[0], self.come[0][0]


def step(*works, name, order=None):
    jobs = [w.job() for w in works]
    outs = [jax.eval_shape(lambda *a, fn=fn: fn(*a), *arrays) for fn, arrays in jobs]

    def body(*refs):
        refs = list(refs)
        ins, results = refs[: sum(len(a) for _, a in jobs)], refs[sum(len(a) for _, a in jobs) :]
        for fn, arrays in jobs:
            values = fn(*[r[...] for r in ins[: len(arrays)]])
            ins = ins[len(arrays) :]
            store(results[: len(values)], values)
            results = results[len(values) :]

    values = call(
        body, [o.shape for out in outs for o in out], *[a for _, arrays in jobs for a in arrays],
        name=name, order=order, flops=1.5e10, vmem=12,
    )
    for w, out in zip(works, outs):
        w.take(values[: len(out)])
        values = values[len(out) :]


def sum_small(a, count):
    small = Small(a, count)
    small.launch()
    while not small.last:
        step(small, name="add")
        small.launch()
    return small.parts()


def shards(
    count,
    features,
    counts,
    cotangent,
    weight_in,
    weight_temp,
    weight_slice,
    weight_qkv,
    weight_out,
    expansion_matrix,
    weight_down,
    weight_head,
):
    n, width = features.shape
    dh, m = weight_slice.shape[1:]
    ff = expansion_matrix.shape[2]
    hm = H * m
    far = lambda *arrays: [Far(a) for a in arrays]
    qkv = lambda l: Far(weight_qkv, l)
    rear_w = lambda l: [Far(w, l) for w in (weight_out, expansion_matrix, weight_down)]
    front_w = lambda l: [Far(weight_in, l), Far(weight_temp), Far(weight_slice, l)]

    kept = [(n, hm), (n, 2 * width), (n, width), (n, 1), (n, hm), (n, hm), (n, width)]
    front_shapes = [(dh + 8, hm)] + [Far(s) for s in kept]
    rear_shapes = [Far(s) for s in [(dh, hm), (n, width), (n, width), (n, 1), (n, ff)]]
    run = lambda *rows: sum(aligned(r // count) for r in rows)
    a1 = run(ff, width // 2)
    a2 = run(ff, width // 2, width)
    a3 = run(width, 8 * count, width)
    chunks = lambda rows: [(count // 2, rows, 256)] * 2
    with_count = lambda body: partial(body, count)

    p0, s0, proj0, nf0, _, lg0, r0, rs0 = call(
        kernel_a, front_shapes, counts, Far(features), *front_w(0), name="front0"
    )
    p0 = sum_small(p0, count)
    mix0, des0, n10, rd10, pre0, f1, p1, s1, proj1, nf1, rstd1, lg1, r1, rs1 = call(
        kernel_b, rear_shapes + [Far((n, width))] + front_shapes,
        counts, *p0, Far(features), Far(s0), qkv(0), *rear_w(0), *front_w(1), name="rear0_front1",
    )
    p1 = sum_small(p1, count)
    pred, g_head, d_first, ds1, dm, keep, send = call(
        with_count(kernel_c),
        [Far((2, n)), (8, width), (n, width), (n, hm), (dh, hm)] + chunks(2 * a1),
        counts, *p1, Far(f1), Far(s1), qkv(1), *rear_w(1), Far(weight_head.T), Far(cotangent),
        name="rear1_head_back1",
    )

    order = Order()

    def advance(*works):
        for w in works:
            if isinstance(w, Small):
                step(w, name="add", order=order)
                w.launch()
            elif w.phase != "last":
                step(w, name="chunks", order=order)
                w.launch()

    dm = Small(dm, count)
    first = Chunks(keep, send, a1, count)
    dm.launch()
    first.launch()
    advance(dm)
    while not dm.last:
        advance(first, dm)

    gq1, ds0, dm0, keep, send = call(
        with_count(kernel_d), [(dh, 3 * dh), (n, hm), (dh + 8, hm)] + chunks(2 * a2),
        *p1, *dm.parts(), qkv(1), g_head, d_first, ds1, *far(s1, proj1, nf1, rstd1, lg1, r1, rs1),
        *front_w(1), *far(s0, mix0, des0, n10, rd10, pre0), *rear_w(0), name="back_front1_rear0",
        order=order,
    )

    dm = Small(dm0, count)
    second = Chunks(keep, send, a2, count)
    dm.launch()
    second.launch()
    advance(first, dm)
    while not dm.last:
        advance(second, dm, first)

    gq0, small1, keep, send = call(
        with_count(kernel_e), [(dh, 3 * dh), (8, hm)] + chunks(a3),
        *p0, *dm.parts(), qkv(0), ds0, *far(s0, proj0, nf0, lg0, r0, rs0), *front_w(0),
        name="back_front0", order=order,
    )
    third = Chunks(keep, send, aligned(width // count) + 8, count)
    third.launch()
    while any(w.phase != "last" for w in (first, second, third)):
        advance(second, first, third)

    *grads, g_head = call(
        with_count(kernel_f),
        [
            (L, width, 2 * width), (L, dh), (L, dh, m), (L, dh, 3 * dh), (L, width, width),
            (L, width, ff), (L, ff, width), (2, width),
        ],
        *first.result(), *second.result(), *third.result(), gq0, gq1, small1,
        name="place_gradients", scratch=[pltpu.VMEM((8 * count, 256), F32)], final=True,
    )
    return (pred, *grads, g_head.T)


def solution(mesh):
    cells = P(("grp", "cell"))
    return jax.shard_map(
        partial(shards, mesh.shape["cell"]),
        mesh=mesh,
        in_specs=(P(("grp", "cell"), None), cells, P(None, ("grp", "cell"))) + (P(),) * 8,
        out_specs=(
            P(None, ("grp", "cell")),
            P("grp", None, None),
            P("grp", None),
            P("grp", None, None),
            P("grp", None, None),
            P("grp", None, None),
            P("grp", None, None),
            P("grp", None, None),
            P("grp", None),
        ),
        check_vma=False,
    )
```

```python
from functools import partial

import jax
import jax.numpy as jnp
from jax import lax
from jax.experimental import pallas as pl
from jax.experimental.pallas import tpu as pltpu
from jax.sharding import PartitionSpec as P

H = 8
L = 2
F32 = jnp.float32
BF16 = jnp.bfloat16
EPS = 1e-05
MIB = 1024 * 1024


def split(a):
    if isinstance(a, tuple):
        return a
    hi = a.astype(BF16)
    return hi, (a - hi.astype(F32)).astype(BF16)


def exact(a):
    return (a.astype(BF16),)


def raw(a, b, ca, cb):
    return lax.dot_general(a, b, (((ca,), (cb,)), ((), ())), preferred_element_type=F32)


def product(a, b, ca, cb):
    a, b = split(a), split(b)
    out = raw(a[0], b[0], ca, cb)
    if len(b) > 1:
        out = out + raw(a[0], b[1], ca, cb)
    if len(a) > 1:
        out = out + raw(a[1], b[0], ca, cb)
    return out


def nn(a, b):
    return product(a, b, 1, 0)


def nt(a, b):
    return product(a, b, 1, 1)


def tn(a, b):
    return product(a, b, 0, 0)


def same_head(rows, row_head, cols, col_head):
    r = lax.broadcasted_iota(jnp.int32, (rows, cols), 0) // row_head
    c = lax.broadcasted_iota(jnp.int32, (rows, cols), 1) // col_head
    return r == c


def ones_block(rows, row_head, cols, col_head):
    return exact(same_head(rows, row_head, cols, col_head).astype(F32))


def expand(small, col_head):
    r, cols = small.shape
    tiled = jnp.concatenate([small] * H, axis=0)
    return jnp.where(same_head(H * r, r, cols, col_head), tiled, 0.0)


def fold(dense, col_head):
    rows, cols = dense.shape
    r = rows // H
    head = lax.broadcasted_iota(jnp.int32, (r, cols), 1) // col_head
    out = jnp.where(head == 0, dense[:r], 0.0)
    for h in range(1, H):
        out = jnp.where(head == h, dense[h * r : (h + 1) * r], out)
    return out


def tile_lanes(a, times):
    return jnp.concatenate([a] * times, axis=1)


def norm(field):
    centered = field - jnp.mean(field, axis=-1, keepdims=True)
    rstd = lax.rsqrt(jnp.mean(centered * centered, axis=-1, keepdims=True) + EPS)
    return centered * rstd, rstd


def norm_back(dy, y, rstd):
    return rstd * (
        dy - jnp.mean(dy, axis=-1, keepdims=True) - y * jnp.mean(dy * y, axis=-1, keepdims=True)
    )


def softplus(t):
    return jnp.maximum(t, 0.0) + jnp.log(1.0 + jnp.exp(-jnp.abs(t)))


def front(field, w_in, w_temp, w_slice, live):
    n, width = field.shape
    dh, m = w_slice.shape
    hm = H * m
    nf, rstd = norm(field)
    proj = nn(nf, w_in)
    x, v = proj[:, :width], proj[:, width:]
    wt = tile_lanes(w_temp, H)
    xt = split(x * wt)
    t_wide = nn(xt, ones_block(width, dh, hm, m))
    t_slim = nn(xt, ones_block(width, dh, width, dh))
    r = 1.0 / (0.5 + softplus(t_wide))
    rs = jax.nn.sigmoid(t_slim) / (0.5 + softplus(t_slim))
    logits = nn(x, expand(tile_lanes(w_slice, H), m)) * r
    e = jnp.exp(logits)
    z = nn(e, ones_block(hm, m, hm, m))
    rows = lax.broadcasted_iota(jnp.int32, (n, hm), 0)
    s = jnp.where(rows < live, e / z, 0.0)
    numer = fold(tn(v, s), m)
    denom = jnp.sum(s, axis=0, keepdims=True)
    packed = jnp.concatenate([numer, jnp.broadcast_to(denom, (8, hm))], axis=0)
    return packed, s, proj, nf, rstd, logits, r, rs


def tokens_of(packed, dh):
    inv = 1.0 / (packed[dh : dh + 1] + EPS)
    return packed[:dh] * inv, inv


def middle(packed, w_qkv):
    dh = w_qkv.shape[0]
    tok, inv = tokens_of(packed, dh)
    qkv = tn(w_qkv, tok)
    q, k, v = qkv[:dh], qkv[dh : 2 * dh], qkv[2 * dh :]
    hm = tok.shape[1]
    m = hm // H
    pair = 2 * m
    own = same_head(pair, m, pair, m)
    scale = 1.0 / float(dh) ** 0.5
    maps, mixed = [], []
    for g in range(H // 2):
        lanes = slice(g * pair, (g + 1) * pair)
        e = jnp.where(own, jnp.exp(tn(k[:, lanes], q[:, lanes]) * scale), 0.0)
        a = e / jnp.sum(e, axis=0, keepdims=True)
        maps.append(a)
        mixed.append(nn(v[:, lanes], a))
    return tok, inv, q, k, v, maps, jnp.concatenate(mixed, axis=1)


def middle_back(packed, w_qkv, d_mixed):
    dh = w_qkv.shape[0]
    tok, inv, q, k, v, maps, _ = middle(packed, w_qkv)
    hm = tok.shape[1]
    pair = 2 * (hm // H)
    scale = 1.0 / float(dh) ** 0.5
    dq, dk, dv = [], [], []
    for g in range(H // 2):
        lanes = slice(g * pair, (g + 1) * pair)
        a, dm = maps[g], d_mixed[:, lanes]
        dv.append(nt(dm, a))
        da = tn(v[:, lanes], dm)
        ds = a * (da - jnp.sum(a * da, axis=0, keepdims=True)) * scale
        dk.append(nt(q[:, lanes], ds))
        dq.append(nn(k[:, lanes], ds))
    d_qkv = jnp.concatenate([jnp.concatenate(p, axis=1) for p in (dq, dk, dv)], axis=0)
    g_qkv = nt(tok, d_qkv)
    d_tok = nn(w_qkv, d_qkv)
    d_numer = d_tok * inv
    d_denom = -jnp.sum(d_tok * tok, axis=0, keepdims=True) * inv
    return g_qkv, d_numer, d_denom


def front_back(ds, d_numer, d_denom, s, proj, nf, logits, r, rs, w_in, w_temp, w_slice):
    width = proj.shape[1] // 2
    dh, m = w_slice.shape
    hm = H * m
    x, v = proj[:, :width], proj[:, width:]
    d_blk = split(expand(d_numer, m))
    ds = ds + nn(v, d_blk) + d_denom
    dv = nt(s, d_blk)
    sds = s * ds
    d_logits = sds - s * nn(sds, ones_block(hm, m, hm, m))
    d_t = -rs * nn(d_logits * logits, ones_block(hm, m, width, dh))
    du = split(d_logits * r)
    wt = tile_lanes(w_temp, H)
    dx = nt(du, expand(tile_lanes(w_slice, H), m)) + d_t * wt
    g_temp = jnp.sum(x * d_t, axis=0, keepdims=True)
    g_slice = fold(tn(x, du), m)
    g_slice = sum(g_slice[:, g * 2 * m : (g + 1) * 2 * m] for g in range(H // 2))
    g_slice = g_slice[:, :m] + g_slice[:, m:]
    d_proj = split(jnp.concatenate([dx, dv], axis=1))
    g_in = tn(nf, d_proj)
    return d_proj, g_in, g_temp, g_slice


def gelu_parts(pre):
    c = 0.7978845608028654
    sq = pre * pre
    t = jnp.tanh(c * pre * (1.0 + 0.044715 * sq))
    hid = 0.5 * pre * (1.0 + t)
    slope = 0.5 * (1.0 + t) + 0.5 * pre * (1.0 - t * t) * c * (1.0 + 3 * 0.044715 * sq)
    return hid, slope


def rear(field, s, mixed, w_out, w_up, w_down):
    m = mixed.shape[1] // H
    des = nt(s, expand(mixed, m))
    first = field + nn(des, w_out)
    n1, rstd1 = norm(first)
    pre = nn(n1, w_up)
    hid, _ = gelu_parts(pre)
    return first + nn(hid, w_down), des, n1, rstd1, pre


def rear_back(g, s, mixed, des, n1, rstd1, pre, w_out, w_up, w_down):
    m = mixed.shape[1] // H
    hid, slope = gelu_parts(pre)
    gs = split(g)
    g_down = tn(hid, gs)
    d_pre = split(nt(gs, w_down) * slope)
    g_up = tn(n1, d_pre)
    d_first = g + norm_back(nt(d_pre, w_up), n1, rstd1)
    dfs = split(d_first)
    g_out = tn(des, dfs)
    d_des = split(nt(dfs, w_out))
    ds = nn(d_des, expand(mixed, m))
    d_mixed = fold(tn(d_des, s), m)
    return d_first, ds, d_mixed, g_out, g_up, g_down


def aligned(rows):
    return -(-rows // 8) * 8


def slabs(value):
    return [value[:, i : i + 256] for i in range(0, value.shape[1], 256)]


def scatter(count, pieces, keep, send):
    me = lax.axis_index("cell")
    core = lax.rem(me, 2)

    def put(mine, other):
        for c in range(count):
            slot = (c ^ me) // 2
            at = 0
            for piece in pieces:
                rows = sum(p.shape[0] for p in piece) // count
                which, start = divmod(c * rows, piece[0].shape[0])
                ref = mine if c % 2 == 0 else other
                ref[slot, at : at + rows] = piece[which][start : start + rows]
                at += aligned(rows)

    pl.when(core == 0)(lambda: put(keep, send))
    pl.when(core == 1)(lambda: put(send, keep))


def gather(count, own, other, pieces):
    me = lax.axis_index("cell")
    core = lax.rem(me, 2)

    def take(mine, theirs):
        for c in range(count):
            slot = (c ^ me) // 2
            at = 0
            for rows, targets in pieces:
                each = rows // count
                which, start = divmod(c * each, rows // len(targets))
                src = mine if c % 2 == 0 else theirs
                targets[which](start, src[slot, at : at + each])
                at += aligned(each)

    pl.when(core == 0)(lambda: take(own, other))
    pl.when(core == 1)(lambda: take(other, own))


def into(ref, layer, column, base=0):
    def write(start, value):
        start = base + start
        ref[layer, start : start + value.shape[0], column : column + 256] = value

    return write


def rows_of(ref):
    def write(start, value):
        ref[start : start + value.shape[0]] = value

    return write


def store(refs, values):
    for ref, value in zip(refs, values, strict=True):
        ref[...] = value


def pack_small(g_temp, g_slice, g_head, hm):
    dh, m = g_slice.shape
    width = g_temp.shape[1]
    left = jnp.concatenate([g_temp, g_head, jnp.zeros((8 - 3, width), F32)], axis=0)
    run = dh // 8
    right = jnp.concatenate([g_slice[i * 8 : i * 8 + 8] for i in range(run)], axis=1)
    return left, right


def kernel_a(live, field, w_in, w_temp, w_slice, *out):
    store(out, front(field[...], w_in[...], w_temp[0:1], w_slice[...], live[0]))


def kernel_b(live, pa, pb, field, s, w_qkv, w_out, w_up, w_down, w_in, w_temp, w_slice, *out):
    mixed = middle(pa[...] + pb[...], w_qkv[...])[-1]
    f1, des, n1, rstd1, pre = rear(field[...], s[...], mixed, w_out[...], w_up[...], w_down[...])
    store(out[:5], (mixed, des, n1, rstd1, pre))
    out[5][...] = f1
    store(out[6:], front(f1, w_in[...], w_temp[1:2], w_slice[...], live[0]))


def kernel_c(count, live, pa, pb, field, s, w_qkv, w_out, w_up, w_down, w_head, cot, *out):
    pred, g_head, d_first, ds, d_mixed, keep, send = out
    n, width = field.shape
    mixed = middle(pa[...] + pb[...], w_qkv[...])[-1]
    s = s[...]
    f2, des, n1, rstd1, pre = rear(field[...], s, mixed, w_out[...], w_up[...], w_down[...])
    n2, rstd2 = norm(f2)
    wh = jnp.concatenate([w_head[...], jnp.zeros((6, width), F32)], axis=0)
    n2s = split(n2)
    pred[...] = nt(wh, n2s)[:2]
    lanes = lax.broadcasted_iota(jnp.int32, cot.shape, 1)
    dp = jnp.where(lanes < live[0], cot[...], 0.0)
    dp = jnp.concatenate([dp, jnp.zeros((6, n), F32)], axis=0)
    g_head[...] = nn(dp, n2s)
    g = norm_back(tn(dp, wh), n2, rstd2)
    d_first[...], ds[...], d_mixed[...], g_out, g_up, g_down = rear_back(
        g, s, mixed, des, n1, rstd1, pre, w_out[...], w_up[...], w_down[...]
    )
    halves = [g_out[: width // 2], g_out[width // 2 :]]
    scatter(count, [[g_down], [halves[0]], slabs(g_up), [halves[1]]], keep, send)


def kernel_d(
    count, pa, pb, ma, mb, w_qkv, g_head, d_first, ds, s, proj, nf, rstd, logits, r, rs,
    w_in, w_temp, w_slice, s0, mixed0, des0, n10, rstd10, pre0, w_out0, w_up0, w_down0,
    g_qkv, ds0, d_mixed0, g_in1, keep, send,
):
    width = nf.shape[1]
    g_qkv[...], d_numer, d_denom = middle_back(pa[...] + pb[...], w_qkv[...], ma[...] + mb[...])
    d_proj, g_in1[...], g_temp, g_slice = front_back(
        ds[...], d_numer, d_denom, s[...], proj[...], nf[...], logits[...], r[...], rs[...],
        w_in[...], w_temp[1:2], w_slice[...],
    )
    g = d_first[...] + norm_back(nt(d_proj, w_in[...]), nf[...], rstd[...])
    _, ds0[...], d_mixed, g_out, g_up, g_down = rear_back(
        g, s0[...], mixed0[...], des0[...], n10[...], rstd10[...], pre0[...],
        w_out0[...], w_up0[...], w_down0[...],
    )
    left, right = pack_small(g_temp, g_slice, g_head[:2], None)
    d_mixed0[...] = jnp.concatenate([d_mixed, jnp.concatenate([left, right], axis=1)], axis=0)
    halves = [g_out[: width // 2], g_out[width // 2 :]]
    scatter(count, [[g_down], [halves[0]], slabs(g_up), [halves[1]]], keep, send)


def kernel_e(
    count, pa, pb, ma, mb, g_in1, w_qkv, ds, s, proj, nf, logits, r, rs, w_in, w_temp, w_slice,
    g_qkv, small, keep, send,
):
    dh = w_qkv.shape[0]
    dm = ma[...] + mb[...]
    small[...] = dm[dh:]
    g_qkv[...], d_numer, d_denom = middle_back(pa[...] + pb[...], w_qkv[...], dm[:dh])
    _, g_in, g_temp, g_slice = front_back(
        ds[...], d_numer, d_denom, s[...], proj[...], nf[...], logits[...], r[...], rs[...],
        w_in[...], w_temp[0:1], w_slice[...],
    )
    left, right = pack_small(g_temp, g_slice, jnp.zeros((2, g_temp.shape[1]), F32), None)
    rest = jnp.zeros((8 * count - 16, g_temp.shape[1]), F32)
    ins, ins1 = slabs(g_in), slabs(g_in1[...])
    small = jnp.concatenate([left, right, rest], axis=0)
    scatter(count, [[ins[0]], [small], [ins1[0]], [ins[1]], [ins1[1]]], keep, send)


def kernel_f(
    count, own1, oth1, own2, oth2, own3, oth3, gq0, gq1, small1,
    g_in, g_temp, g_slice, g_qkv, g_out, g_up, g_down, g_head, small0,
):
    width = g_out.shape[1]
    dh, m = g_slice.shape[1:]
    ff = g_up.shape[2]

    def down(l):
        return ff, [into(g_down, l, 0)]

    def up(l):
        return width * (ff // 256), [into(g_up, l, i) for i in range(0, ff, 256)]

    def out(l, part):
        return width // 2, [into(g_out, l, 0, part * (width // 2))]

    def ins(l, part):
        return width, [into(g_in, l, part * width)]

    gather(count, own1, oth1, [down(1), out(1, 0), up(1), out(1, 1)])
    gather(count, own2, oth2, [down(0), out(0, 0), up(0), out(0, 1)])
    small = (8 * count, [rows_of(small0)])
    gather(count, own3, oth3, [ins(0, 0), small, ins(1, 0), ins(0, 1), ins(1, 1)])
    g_qkv[0] = gq0[...]
    g_qkv[1] = gq1[...]
    for l, (left, right) in enumerate(
        ((small0[:8], small0[8:16]), (small1[:, :width], small1[:, width:]))
    ):
        g_temp[l : l + 1] = sum(left[:1, h * dh : (h + 1) * dh] for h in range(H))
        for i in range(dh // 8):
            g_slice[l, i * 8 : i * 8 + 8] = right[:, i * m : (i + 1) * m]
    g_head[...] = small1[1:3, :width]


VM = pl.BlockSpec(memory_space=pltpu.VMEM)
SM = pl.BlockSpec(memory_space=pltpu.SMEM)
HBM = pl.BlockSpec(memory_space=pltpu.HBM)


class Fetched:
    def __init__(self, source, target, sem):
        self.copy = pltpu.make_async_copy(source, target, sem)
        self.copy.start()
        self.target, self.waiting = target, True
        self.shape = target.shape

    def finish(self):
        if self.waiting:
            self.copy.wait()
            self.waiting = False

    def __getitem__(self, index):
        self.finish()
        return self.target[index]


class Emitted:
    def __init__(self, source, target, sem):
        self.copy = pltpu.make_async_copy(source, target, sem)
        self.source, self.started = source, False
        self.shape = source.shape

    def __setitem__(self, index, value):
        self.source[index] = value
        if index is Ellipsis:
            self.start()

    def start(self):
        self.copy.start()
        self.started = True

    def finish(self):
        if not self.started:
            self.copy.start()
        self.copy.wait()


class Far:
    def __init__(self, what, layer=None):
        self.what, self.layer = what, layer


class Order:
    def __init__(self):
        self.token = None


def call(body, shapes, *args, name, order=None, scratch=(), flops=1.5e10, vmem=24, final=False):
    specs, arrays, held, far_in, far_out, out_specs, out_shapes = [], [], [], [], [], [], []
    if order is not None:
        inner, tokens = body, int(order.token is not None)
        args = args + (order.token,) * tokens
        used = len(args) - tokens
        shapes = list(shapes) + [(8, 128)]
        results = len(shapes) - 1

        def body(*refs):
            outs = refs[used + tokens :]
            outs[results][...] = jnp.zeros((8, 128), F32)
            inner(*refs[:used], *outs[:results], *outs[results + 1 :])

    for a in args:
        if isinstance(a, Far):
            far_in.append((len(arrays), a.layer))
            held.append(pltpu.VMEM(a.what.shape if a.layer is None else a.what.shape[1:], F32))
            specs.append(HBM)
            a = pltpu.with_memory_space_constraint(a.what, pltpu.HBM)
        else:
            specs.append(SM if a.dtype == jnp.int32 else VM)
            if a.dtype != jnp.int32:
                a = pltpu.with_memory_space_constraint(a, pltpu.VMEM)
        arrays.append(a)
    for s in shapes:
        if isinstance(s, Far):
            far_out.append(len(arrays) + len(out_shapes))
            held.append(pltpu.VMEM(s.what, F32))
            s = s.what
            out_specs.append(HBM)
            out_shapes.append(pltpu.HBM(s, F32))
        else:
            out_specs.append(VM)
            out_shapes.append(jax.ShapeDtypeStruct(s, F32) if final else pltpu.VMEM(s, F32))
    count = len(arrays) + len(shapes)
    copies = len(held)

    def whole(*refs):
        own, extra = list(refs[:count]), refs[count:]
        moved = []
        for at, layer in far_in:
            i = len(moved)
            source = own[at] if layer is None else own[at].at[layer]
            own[at] = Fetched(source, extra[i], extra[copies].at[i])
            moved.append(own[at])
        for at in far_out:
            i = len(moved)
            own[at] = Emitted(extra[i], own[at], extra[copies].at[i])
            moved.append(own[at])
        body(*own, *extra[copies + bool(copies) :])
        for m in moved:
            m.finish()

    if held:
        held.append(pltpu.SemaphoreType.DMA((copies,)))
    values = pl.pallas_call(
        whole,
        out_shape=out_shapes,
        in_specs=specs,
        out_specs=out_specs,
        scratch_shapes=held + list(scratch),
        compiler_params=pltpu.CompilerParams(vmem_limit_bytes=vmem * MIB),
        cost_estimate=pl.CostEstimate(
            flops=int(flops), bytes_accessed=int(flops / 100), transcendentals=0
        ),
        name=name,
    )(*arrays)
    if order is not None:
        order.token = values[-1]
        values = values[:-1]
    return values


def swap(a, bit, count):
    return lax.ppermute(a, "cell", [(i, i ^ bit) for i in range(count)])


def masks_of(group):
    masks = [0]
    for bit in group:
        masks += [m | bit for m in masks]
    return masks


def pairs(count):
    bits = [1 << i for i in range(1, count.bit_length() - 1)]
    return [tuple(bits[i : i + 2]) for i in range(0, len(bits), 2)]


class Small:
    def __init__(self, a, count):
        self.a, self.count = a, count
        self.groups = [(1,)] + pairs(count)

    def launch(self):
        self.come = [swap(self.a, m, self.count) for m in masks_of(self.groups[0])[1:]]

    def job(self):
        def add(a, *come):
            if len(come) == 1:
                return [a + come[0]]
            return [(a + come[0]) + (come[1] + come[2])]

        return add, [self.a, *self.come]

    def take(self, values):
        (self.a,) = values
        self.groups = self.groups[1:]

    @property
    def last(self):
        return len(self.groups) == 1

    def parts(self):
        if len(self.come) == 1:
            return self.a, self.come[0]
        return self.a + self.come[0], self.come[1] + self.come[2]


class Chunks:
    def __init__(self, keep, send, a_rows, count):
        self.count = count
        rows = keep.shape[1]
        groups = pairs(count)
        bits = sorted((b for g in groups for b in g), reverse=True)
        if a_rows is None:
            self.sizes, plans = [rows], [groups]
        else:
            self.sizes = [a_rows, rows - a_rows]
            plans = [[(b,) for g in groups for b in g], [(b,) for g in groups for b in g[::-1]]]
        self.stages = list(zip(*plans))
        self.at, self.phase = 0, "core"
        self.have, self.sends = [keep], [[(send, 1)]]
        self.left = [list(bits) for _ in self.sizes]
        self.bits = bits

    def launch(self):
        self.come = [[swap(a, m, self.count) for a, m in sends] for sends in self.sends]

    @property
    def done(self):
        return self.phase == "done"

    def job(self):
        sizes, left, phase, at, stages = self.sizes, self.left, self.phase, self.at, self.stages
        shapes = [len(c) for c in self.come]
        flat = [x for h, c in zip(self.have, self.come) for x in (h, *c)]

        def unflatten(flat):
            flat, out = list(flat), []
            for k in shapes:
                out.append((flat[0], flat[1 : k + 1]))
                flat = flat[k + 1 :]
            return out

        def rows_split(parts):
            if len(parts) == len(sizes):
                return parts
            a = sizes[0]
            return [parts[0][..., :a, :], parts[0][..., a:, :]]

        def cut(parts, stage):
            out = []
            same = len(parts) == 2 and stage[0] == stage[1]
            if same:
                parts = [jnp.concatenate(parts, axis=-2)]
            for p, l, group in zip(parts, left, stage):
                for mask in masks_of(group):
                    piece, rest = p, list(l)
                    for bit in group:
                        axis = rest.index(bit)
                        piece = lax.index_in_dim(piece, int(mask & bit > 0), axis, keepdims=False)
                        rest.remove(bit)
                    out.append(piece)
            return out

        def summed(flat):
            out = []
            for h, c in unflatten(flat):
                for x in c:
                    h = h + x
                out.append(h)
            return out

        def reduce(*flat):
            parts = summed(flat)
            if phase == "core":
                parts = [parts[0].reshape((2,) * len(left[0]) + parts[0].shape[1:])]
                parts = rows_split(parts)
            if at < len(stages):
                return cut(parts, stages[at])
            return parts

        def gather_one(*flat):
            out = []
            stage = stages[at]
            for (h, c), l, group in zip(unflatten(flat), left, stage):
                done = list(l)
                pieces = dict(zip(masks_of(group), (h, *c)))
                for bit in reversed(group):
                    done = sorted(done + [bit], reverse=True)
                    axis = done.index(bit)
                    pieces = {
                        m: jnp.stack([v, pieces[m | bit]], axis=axis)
                        for m, v in pieces.items()
                        if not m & bit
                    }
                out.append(pieces[0])
            if at == 0:
                if len(out) == 2:
                    out = [jnp.concatenate(out, axis=-2)]
                return [out[0].reshape((-1,) + out[0].shape[-2:])]
            before = stages[at - 1]
            if len(out) == 1 and len(sizes) == 2 and before[0] != before[1]:
                out = rows_split(out)
            return out

        return (gather_one if phase == "gather" else reduce), flat

    def take(self, values):
        values = list(values)
        if self.phase in ("core", "reduce"):
            if self.at < len(self.stages):
                stage = self.stages[self.at]
                self.have, self.sends = [], []
                same = len(stage) == 2 and stage[0] == stage[1]
                for group in stage[:1] if same else stage:
                    masks = masks_of(group)
                    self.have.append(values[0])
                    self.sends.append(list(zip(values[1 : len(masks)], masks[1:])))
                    values = values[len(masks) :]
                self.left = [[b for b in l if b not in g] for l, g in zip(self.left, stage)]
                self.at += 1
                self.phase = "reduce"
                return
            self.phase = "gather"
            self.at -= 1
        else:
            stage = self.stages[self.at]
            self.left = [sorted(l + list(g), reverse=True) for l, g in zip(self.left, stage)]
            self.at -= 1
        self.have = values
        if self.at < 0:
            self.phase = "last"
            self.sends = [[(values[0], 1)]]
        else:
            stage = self.stages[self.at]
            self.sends = [
                [(v, m) for m in masks_of(g)[1:]] for v, g in zip(values, stage)
            ]

    def result(self):
        return self.have[0], self.come[0][0]


def step(*works, name, order=None):
    jobs = [w.job() for w in works]
    outs = [jax.eval_shape(lambda *a, fn=fn: fn(*a), *arrays) for fn, arrays in jobs]

    def body(*refs):
        refs = list(refs)
        ins, results = refs[: sum(len(a) for _, a in jobs)], refs[sum(len(a) for _, a in jobs) :]
        for fn, arrays in jobs:
            values = fn(*[r[...] for r in ins[: len(arrays)]])
            ins = ins[len(arrays) :]
            store(results[: len(values)], values)
            results = results[len(values) :]

    values = call(
        body, [o.shape for out in outs for o in out], *[a for _, arrays in jobs for a in arrays],
        name=name, order=order, flops=1.5e10, vmem=12,
    )
    for w, out in zip(works, outs):
        w.take(values[: len(out)])
        values = values[len(out) :]


def sum_small(a, count):
    small = Small(a, count)
    small.launch()
    while not small.last:
        step(small, name="add")
        small.launch()
    return small.parts()


def shards(
    count,
    features,
    counts,
    cotangent,
    weight_in,
    weight_temp,
    weight_slice,
    weight_qkv,
    weight_out,
    expansion_matrix,
    weight_down,
    weight_head,
):
    n, width = features.shape
    dh, m = weight_slice.shape[1:]
    ff = expansion_matrix.shape[2]
    hm = H * m
    far = lambda *arrays: [Far(a) for a in arrays]
    qkv = lambda l: Far(weight_qkv, l)
    rear_w = lambda l: [Far(w, l) for w in (weight_out, expansion_matrix, weight_down)]
    front_w = lambda l: [Far(weight_in, l), Far(weight_temp), Far(weight_slice, l)]

    kept = [(n, hm), (n, 2 * width), (n, width), (n, 1), (n, hm), (n, hm), (n, width)]
    front_shapes = [(dh + 8, hm)] + [Far(s) for s in kept]
    rear_shapes = [Far(s) for s in [(dh, hm), (n, width), (n, width), (n, 1), (n, ff)]]
    run = lambda *rows: sum(aligned(r // count) for r in rows)
    a1 = run(ff, width // 2)
    a2 = run(ff, width // 2)
    a3 = run(width, 8 * count, width)
    b3 = run(width, width)
    chunks = lambda rows: [(count // 2, rows, 256)] * 2
    with_count = lambda body: partial(body, count)

    p0, s0, proj0, nf0, _, lg0, r0, rs0 = call(
        kernel_a, front_shapes, counts, Far(features), *front_w(0), name="front0"
    )
    p0 = sum_small(p0, count)
    mix0, des0, n10, rd10, pre0, f1, p1, s1, proj1, nf1, rstd1, lg1, r1, rs1 = call(
        kernel_b, rear_shapes + [Far((n, width))] + front_shapes,
        counts, *p0, Far(features), Far(s0), qkv(0), *rear_w(0), *front_w(1), name="rear0_front1",
    )
    p1 = sum_small(p1, count)
    pred, g_head, d_first, ds1, dm, keep, send = call(
        with_count(kernel_c),
        [Far((2, n)), (8, width), (n, width), (n, hm), (dh, hm)] + chunks(2 * a1),
        counts, *p1, Far(f1), Far(s1), qkv(1), *rear_w(1), Far(weight_head.T), Far(cotangent),
        name="rear1_head_back1",
    )

    order = Order()

    def advance(*works):
        for w in works:
            if isinstance(w, Small):
                step(w, name="add", order=order)
                w.launch()
            elif w.phase != "last":
                step(w, name="chunks", order=order)
                w.launch()

    dm = Small(dm, count)
    first = Chunks(keep, send, a1, count)
    dm.launch()
    first.launch()
    advance(dm)
    while not dm.last:
        advance(first, dm)

    gq1, ds0, dm0, g_in1, keep, send = call(
        with_count(kernel_d),
        [(dh, 3 * dh), (n, hm), (dh + 8, hm), (width, 2 * width)] + chunks(2 * a2),
        *p1, *dm.parts(), qkv(1), g_head, d_first, ds1, *far(s1, proj1, nf1, rstd1, lg1, r1, rs1),
        *front_w(1), *far(s0, mix0, des0, n10, rd10, pre0), *rear_w(0), name="back_front1_rear0",
        order=order,
    )

    dm = Small(dm0, count)
    second = Chunks(keep, send, a2, count)
    dm.launch()
    second.launch()
    advance(first, dm)
    while not dm.last:
        advance(second, dm, first)

    gq0, small1, keep, send = call(
        with_count(kernel_e), [(dh, 3 * dh), (8, hm)] + chunks(a3 + b3),
        *p0, *dm.parts(), g_in1, qkv(0), ds0, *far(s0, proj0, nf0, lg0, r0, rs0), *front_w(0),
        name="back_front0", order=order,
    )
    third = Chunks(keep, send, a3, count)
    third.launch()
    while any(w.phase != "last" for w in (first, second, third)):
        advance(second, first, third)

    *grads, g_head = call(
        with_count(kernel_f),
        [
            (L, width, 2 * width), (L, dh), (L, dh, m), (L, dh, 3 * dh), (L, width, width),
            (L, width, ff), (L, ff, width), (2, width),
        ],
        *first.result(), *second.result(), *third.result(), gq0, gq1, small1,
        name="place_gradients", scratch=[pltpu.VMEM((8 * count, 256), F32)], final=True,
    )
    return (pred, *grads, g_head.T)


def solution(mesh):
    cells = P(("grp", "cell"))
    return jax.shard_map(
        partial(shards, mesh.shape["cell"]),
        mesh=mesh,
        in_specs=(P(("grp", "cell"), None), cells, P(None, ("grp", "cell"))) + (P(),) * 8,
        out_specs=(
            P(None, ("grp", "cell")),
            P("grp", None, None),
            P("grp", None),
            P("grp", None, None),
            P("grp", None, None),
            P("grp", None, None),
            P("grp", None, None),
            P("grp", None, None),
            P("grp", None),
        ),
        check_vma=False,
    )
```
